32 devices in a mesh: blk: 4 (over y, core), dp: 8 (over z, x).
Axes of the slice: x: 2, y: 2, z: 4, core: 2. Of those that a mesh axis runs over, the one named last changes fastest.
Arguments:
- fingerprints: bfloat16 [12288, 2048], P(('blk', 'dp')), may hold values from 0 to 3, as said below
- w_first: bfloat16 [2048, 1024], replicated, may hold values from -0.3125 to 0.3125
- w_second: bfloat16 [1024, 512], replicated, may hold values from -0.0625 to 0.0625
Outputs:
- grad_first: float32 [2048, 1024], P('dp')
- grad_second: float32 [1024, 512], P('dp')
The draws below stay inside these ranges and needn't reach their ends.
Inputs may be any that keep to these rules, and one draw needn't show every extreme that they name: `fingerprints`: Non-negative feature weights; every molecule has a third or more of its features nonzero.
All inputs are finite; a program needn't handle non-finite values.
Results may differ from the reference program's by a relative error of at most 0.003.
Values may be sent and summed in bfloat16 or wider, within the bound.
No kernel may reach another device: no remote copies, remote signals or barrier semaphores. Data moves between devices by JAX's collectives and lax.ppermute only.
A program may use at most 64 MiB of HBM per device.

```python
import math
import jax
import jax.numpy as jnp
from jax import lax

D_IN = 2048
HID = 1024
EMB = 512
TOK_DEV = 384
GROUP = 1536
MOLS = 12288
N_BLK = 4
N_DP = 8


def draw_fingerprints(key, part):
    keys = jax.random.split(jax.random.fold_in(key, 11), 9)
    scaffolds = max(GROUP // 24, 4)
    member = jax.random.randint(keys[0], (MOLS,), 0, scaffolds).astype(jnp.int32)
    scaffold_present = jax.random.uniform(keys[1], (scaffolds, D_IN), jnp.float32) < 0.45
    scaffold_mag = jnp.exp(jax.random.uniform(keys[2], (scaffolds, D_IN), jnp.float32, math.log(0.05), 0.0))
    own_mag = jnp.exp(jax.random.uniform(keys[8], (MOLS, D_IN), jnp.float32, math.log(0.05), 0.0))
    column = jnp.exp(jax.random.uniform(keys[3], (1, D_IN), jnp.float32, -1.0, 1.0))
    keep = jax.random.uniform(keys[4], (MOLS, D_IN), jnp.float32) < 0.85
    own_density = jax.random.uniform(keys[5], (MOLS, 1), jnp.float32, 0.1, 0.3)
    own_present = jax.random.uniform(keys[6], (MOLS, D_IN), jnp.float32) < own_density
    jitter = jax.random.uniform(keys[7], (MOLS, D_IN), jnp.float32, 0.8, 1.1)
    shared_present = jnp.take(scaffold_present, member, axis=0) & keep
    shared_mag = jnp.take(scaffold_mag, member, axis=0) * jitter
    values = jnp.where(shared_present, shared_mag, jnp.where(own_present, own_mag, 0.0))
    values = values * column
    return values.astype(jnp.bfloat16)


def centred(stream_key, extent, spread, limit, dtype=jnp.bfloat16):
    result = jax.random.normal(stream_key, extent, jnp.float32) * spread
    return jnp.minimum(jnp.maximum(result, -limit), limit).astype(dtype)


def setup_inputs(seed: int = 0) -> dict:
    streams_of = jax.random.split(jax.random.key(seed), 4)
    fingerprints = draw_fingerprints(jax.random.fold_in(streams_of[3], 71), 0)
    w_first = centred(streams_of[1], (D_IN, HID), 0.05, 0.3125)
    w_second = centred(streams_of[2], (HID, EMB), 0.01, 0.0625)
    return {"fingerprints": fingerprints, "w_first": w_first, "w_second": w_second}


def group_terms(pair):
    feats, embeds = pair
    sqn = lax.optimization_barrier(jnp.sum(jnp.square(feats.astype(jnp.float32)), axis=1))
    inter = jnp.dot(feats, feats.T, preferred_element_type=jnp.float32)
    tanimoto = inter / (sqn[:, None] + sqn[None, :] - inter)
    pred = jnp.dot(embeds, embeds.T, preferred_element_type=jnp.float32) * (1.0 / math.sqrt(EMB))
    resid = (pred - tanimoto).astype(jnp.bfloat16)
    return jnp.dot(resid, embeds, preferred_element_type=jnp.float32)

def reference(fingerprints, w_first, w_second):
    pre = jnp.dot(fingerprints, w_first, preferred_element_type=jnp.float32)
    sig = jax.nn.sigmoid(pre)
    hidden = (pre * sig).astype(jnp.bfloat16)
    embed = jnp.dot(hidden, w_second, preferred_element_type=jnp.float32).astype(jnp.bfloat16)
    feats = fingerprints.reshape(N_BLK, N_DP, TOK_DEV, D_IN).transpose(1, 0, 2, 3).reshape(N_DP, GROUP, D_IN)
    embeds = embed.reshape(N_BLK, N_DP, TOK_DEV, EMB).transpose(1, 0, 2, 3).reshape(N_DP, GROUP, EMB)
    summed = lax.map(group_terms, (feats, embeds))
    summed = summed.reshape(N_DP, N_BLK, TOK_DEV, EMB).transpose(1, 0, 2, 3).reshape(MOLS, EMB)
    dembed = (summed * (2.0 / math.sqrt(GROUP * MOLS))).astype(jnp.bfloat16)
    dhidden = jnp.dot(dembed, w_second.T, preferred_element_type=jnp.float32)
    dpre = (dhidden * sig * (1.0 + pre * (1.0 - sig))).astype(jnp.bfloat16)
    grad_second = jnp.dot(hidden.T, dembed, preferred_element_type=jnp.float32)
    grad_first = jnp.dot(fingerprints.T, dpre, preferred_element_type=jnp.float32)
    return (grad_first, grad_second)
```

```python
import functools
import math

import jax
import jax.numpy as jnp
from jax import lax
from jax.experimental import pallas as pl
from jax.experimental.pallas import tpu as pltpu
from jax.sharding import PartitionSpec as P

F32 = jnp.float32
BF16 = jnp.bfloat16
F16 = jnp.float16
NN = (((1,), (0,)), ((), ()))
NT = (((1,), (1,)), ((), ()))
TN = (((0,), (0,)), ((), ()))
CHUNKS = 3
CUT = 144
VMEM_LIMIT = 20 * 1024 * 1024


def dot(left, right, dims=NN):
    return lax.dot_general(left, right, dims, preferred_element_type=F32)


def blk_swap(value, bit):
    count = lax.axis_size("blk")
    return lax.ppermute(value, "blk", [(b, b ^ bit) for b in range(count)])


def dp_swap(value, bit):
    count = lax.axis_size("dp")
    return lax.ppermute(value, "dp", [(d, d ^ bit) for d in range(count)])


def quarter_of(place, j):
    return pl.multiple_of((place ^ j) * 256, 256)


def encode(place, feats, kept, w_first, w_second, hidden_out, gate_out, acc):
    for j in range(4):
        units = pl.ds(quarter_of(place, j), 256)
        pre = dot(feats[...], w_first[:, units])
        sig = jax.nn.sigmoid(pre)
        hidden = (pre * sig).astype(BF16)
        hidden_out[:, j * 256 : (j + 1) * 256] = hidden[:kept]
        if j < 2:
            gate = sig[:kept] * (1.0 + pre[:kept] * (1.0 - sig[:kept]))
            gate_out[j] = gate.T
        part = dot(hidden, w_second[units, :])
        if j == 0:
            acc[...] = part
        else:
            acc[...] += part
    return acc[...].astype(BF16)


def residual(inter, pred, sq_rows, sq_cols, emb):
    tanimoto = inter / (sq_rows + sq_cols - inter)
    return (pred * (1.0 / math.sqrt(emb)) - tanimoto).astype(BF16)


def first_stage(i, o, s):
    tok, emb = i["own"].shape[0], i["w_second"].shape[1]
    feats = o["feats"]
    feats[:tok] = i["own"][...]
    feats[tok:] = i["sib"][...]
    embed = encode(
        i["place"][0], feats, tok, i["w_first"], i["w_second"], o["hidden"], o["gate"], s["acc"]
    )
    o["embed"][...] = embed
    wide = feats[...].astype(F32)
    sq = jnp.broadcast_to(jnp.sum(wide * wide, axis=1, keepdims=True), o["sq"].shape)
    o["sq"][...] = sq
    sq_cols = sq.T[:1]
    inter = dot(feats[:tok], feats[...], NT)
    pred = dot(embed[:tok], embed, NT)
    resid = residual(inter, pred, sq[:tok, :1], sq_cols, emb)
    o["summed", 0][...] = dot(resid, embed)
    o["token"][...] = jnp.zeros((8, 128), F32)


def add_columns(k, feats, embed, sq, embed_new, summed, emb, tok, part):
    top = feats[k][...]
    inter = dot(top, top, NT)
    at = lax.broadcasted_iota(jnp.int32, inter.shape, 0)
    to = lax.broadcasted_iota(jnp.int32, inter.shape, 1)
    diagonal = jnp.where(at == to, inter, 0.0)
    sq_rows = jnp.sum(diagonal, axis=1, keepdims=True)
    sq_cols = jnp.sum(diagonal, axis=0, keepdims=True)
    sq[k][...] = jnp.broadcast_to(sq_rows, sq[k].shape)
    resid = residual(inter, dot(embed_new, embed_new, NT), sq_rows, sq_cols, emb)
    total = dot(resid[:, :part], embed_new, TN)
    for j in range(k):
        pieces = [(0, tok, True), (tok, tok, False)] if j == 0 else [(0, 2 * part, True)]
        for start, count, keep in pieces:
            rows = pl.ds(start, count)
            old_embed = embed[j][rows, :]
            inter = dot(feats[j][rows, :], top, NT)
            pred = dot(old_embed, embed_new, NT)
            resid = residual(inter, pred, sq[j][rows, :1], sq_cols, emb)
            if keep:
                mine = resid if j == 0 else resid[:part]
                summed[j][...] += dot(mine, embed_new)
            total += dot(resid[:, :part], old_embed, TN)
    return total


def next_stage(k, i, o, s):
    tok, part, emb = i["summed", 0].shape[0], i["rem"].shape[0], i["w_second"].shape[1]
    feats = [i["feats", j] for j in range(k)] + [o["feats"]]
    feats[k][:part] = i["rem"][...]
    half = part // 2
    feats[k][part : part + half] = i["rs", 0][...]
    feats[k][part + half :] = i["rs", 1][...]
    embed = [i["embed", j] for j in range(k)]
    sq = [i["sq", j] for j in range(k)] + [o["sq"]]
    embed_new = encode(
        i["place"][0], feats[k], part, i["w_first"], i["w_second"], o["hidden"], o["gate"], s["acc"]
    )
    o["embed"][...] = embed_new
    summed = [o["summed", j] for j in range(k + 1)]
    for j in range(k):
        summed[j][...] = i["summed", j][...]
    summed[k][...] = add_columns(k, feats, embed, sq, embed_new, summed, emb, tok, part)
    if "token" in o:
        o["token"][...] = jnp.zeros((8, 128), F32)


def last_stage(factor, i, o, s):
    k = CHUNKS
    place = i["place"][0]
    next_stage(k, i, {**s, **o}, s)
    tok, part = i["summed", 0].shape[0], i["rem"].shape[0]
    wide = i["w_second"].shape[1] // 4
    starts = [0] + [tok + part * j for j in range(k)]
    sizes = [tok] + [part] * k
    for j in range(k + 1):
        rows = pl.ds(starts[j], sizes[j])
        piece = (s["summed", j][...] * factor).astype(BF16)
        s["sum_embed"][rows, :] = piece
        for q in range(4):
            s["dembed"][q, rows, :] = piece[:, q * wide : (q + 1) * wide]
    gates = [i["gate", j] for j in range(k)] + [s["gate"]]
    hiddens = [i["hidden", j] for j in range(k)] + [s["hidden"]]
    for n, name in ((1, "give"), (0, "keep")):
        units = pl.ds(quarter_of(place, n), 256)
        turned = dot(i["w_second"][units, :], s["sum_embed"][...], NT)
        for j in range(k + 1):
            rows = slice(starts[j], starts[j] + sizes[j])
            o[name][:, rows] = (turned[:, rows] * gates[j][n]).astype(BF16)
        second_share(place, place ^ n, s["dembed"], hiddens, o["second_" + name])


def second_share(place, quarter, dembed, hiddens, out):
    total, start = None, 0
    for hidden in hiddens:
        count = hidden.shape[0]
        part = dot(dembed[quarter, start : start + count, :], hidden[...], TN)
        total = part if total is None else total + part
        start += count
    for j in range(4):
        out[:, pl.ds(quarter_of(place, j), 256)] = total[:, j * 256 : (j + 1) * 256]


def exponent(bound):
    return jnp.clip(jnp.ceil(jnp.log2(jnp.maximum(bound, 1e-30))) + 1.0, -100.0, 120.0)


def gradients(i, o, s):
    second = i["second_keep"][...] + i["second_got"][...]
    sums = jnp.sum(jnp.abs(i["keep"][...].astype(F32)), axis=1, keepdims=True)
    sums += jnp.sum(jnp.abs(i["got"][...].astype(F32)), axis=1, keepdims=True)
    exp_first = exponent(3.0 * jnp.max(sums, axis=0, keepdims=True))
    most = jnp.max(jnp.abs(second), axis=1, keepdims=True)
    exp_second = exponent(jnp.max(most, axis=0, keepdims=True))
    exp_first = jnp.broadcast_to(exp_first, (8, 256))
    exp_second = jnp.broadcast_to(exp_second, (8, 256))
    one, two = o["one"], o["two"]
    top, bottom = CUT, 256 - CUT
    for d in range(8):
        block = second[:, d * 128 : (d + 1) * 128]
        one[d, top : top + 64, :128] = block[:64]
        one[d, top : top + 64, 128:] = block[64:]
        one[d, top + 64 : top + 72] = exp_first
        one[d, top + 72 :] = exp_second
        two[d, bottom : bottom + 8] = exp_first
        two[d, bottom + 8 :] = exp_first
    o["kind_one"][:top] = jnp.zeros((top, 256), F32)
    o["kind_one"][top : top + 64] = jnp.ones((64, 256), F32)
    o["kind_one"][top + 64 :] = jnp.full((16, 256), 2.0, F32)
    o["kind_two"][:bottom] = jnp.zeros((bottom, 256), F32)
    o["kind_two"][bottom:] = jnp.full((16, 256), 2.0, F32)
    for d in range(8):
        block, at = None, 0
        for j in range(CHUNKS + 1):
            f = i["feats", j]
            count = f.shape[0] // 2
            for half, name in enumerate(("keep", "got")):
                rows = f[half * count : (half + 1) * count, d * 256 : (d + 1) * 256]
                piece = dot(i[name][:, at : at + count], rows)
                block = piece if block is None else block + piece
            at += count
        one[d, :top] = block[:top]
        two[d, :bottom] = block[top:]


def run(body, ins, outs, scratch, limit=VMEM_LIMIT):
    names_in, names_out, names_s = list(ins), list(outs), list(scratch)

    def kernel(*refs):
        n, m = len(names_in), len(names_out)
        i = dict(zip(names_in, refs[:n]))
        o = dict(zip(names_out, refs[n : n + m]))
        body(i, o, dict(zip(names_s, refs[n + m :])))

    vmem = pltpu.VMEM
    spaces = {"place": pltpu.SMEM, "arg": pl.ANY}
    shapes = [jax.ShapeDtypeStruct(*v) for v in outs.values()]
    got = pl.pallas_call(
        kernel,
        out_shape=shapes,
        in_specs=[pl.BlockSpec(memory_space=spaces.get(n, vmem)) for n in names_in],
        out_specs=[pl.BlockSpec(memory_space=vmem)] * len(shapes),
        scratch_shapes=[vmem(*v) if isinstance(v, tuple) else v for v in scratch.values()],
        compiler_params=pltpu.CompilerParams(vmem_limit_bytes=limit),
        cost_estimate=pl.CostEstimate(flops=1, bytes_accessed=1, transcendentals=0),
    )(*ins.values())
    return dict(zip(names_out, got))


def split(i, o, s):
    half = i["rem"].shape[0] // 2
    for h in range(2):
        o["rows", h][...] = i["rem"][h * half : (h + 1) * half]


def fetch(pairs, i, o, s):
    copies = []
    for n, (source, start, count, target) in enumerate(pairs):
        rows = i[source].at[pl.ds(start, count), :]
        copies.append(pltpu.make_async_copy(rows, o[target], s["sems"].at[n]))
        copies[-1].start()
    for copy in copies:
        copy.wait()


def encode16(total, kind, tail):
    first, second = exps_of(total, tail)
    e = jnp.where(kind == 0.0, first, second)
    scale = jnp.where(kind == 2.0, 1.0, jnp.exp2(15.0 - e))
    return (total * scale).astype(F16)


def decode16(got, kind, tail):
    got = got.astype(F32)
    first, second = exps_of(got, tail)
    e = jnp.where(kind == 0.0, first, second)
    return got * jnp.where(kind == 2.0, 1.0, jnp.exp2(e - 15.0))


def exps_of(value, tail):
    rows = value.ndim - 2
    return [lax.slice_in_dim(value, tail + at, tail + at + 1, axis=rows) for at in (0, 8)]


def halves(value, axis, mine):
    low = lax.index_in_dim(value, 0, axis, keepdims=False)
    high = lax.index_in_dim(value, 1, axis, keepdims=False)
    return jnp.where(mine == 0, low, high), jnp.where(mine == 0, high, low)


def pick(total, axis, index):
    return lax.dynamic_index_in_dim(total, index, axis, keepdims=False)


class Sum:
    def __init__(self, total, kind, order):
        self.total, self.kind = total, kind
        self.tail = total.shape[-2] - 16
        self.axes = list(range(total.ndim - 2))
        self.order = order

    def send(self, step, shifts):
        axis = self.order[step]
        at, size = self.axes.index(axis), self.total.shape[self.axes.index(axis)]
        me = (lax.axis_index("dp") >> shifts[axis]) & (size - 1)
        gots = []
        for o in range(1, size):
            give = pick(self.total, at, me ^ o)
            gots.append(dp_swap(encode16(give, self.kind, self.tail), o << shifts[axis]))
        self.axes.pop(at)
        self.keep = pick(self.total, at, me)
        return gots

    def receive(self, gots):
        others = [decode16(g, self.kind, self.tail) for g in gots]
        total, top = self.keep, self.keep
        for other in others:
            total = total + other
            top = jnp.maximum(top, other)
        self.total = jnp.where(self.kind == 2.0, top + float(len(others)), total)


def split_lanes(packed, bounds, count):
    if count == 1:
        return packed
    blocks, rows, lanes = packed.shape
    plain = packed.reshape(blocks, rows, count, lanes // count)
    paired = packed.reshape(blocks, rows, 2, count, lanes // 2 // count)
    plain = jnp.moveaxis(plain, 2, 1)
    paired = jnp.moveaxis(paired, 3, 1).reshape(plain.shape)
    row = lax.broadcasted_iota(jnp.int32, plain.shape, 2)
    both = jnp.where((row >= bounds[0]) & (row < bounds[1]), paired, plain)
    return both.reshape(blocks * count, rows, lanes // count)


def per_device(fingerprints, w_first, w_second):
    tok, width = fingerprints.shape
    hid, emb = w_second.shape
    blk_count = lax.axis_size("blk")
    dp_count = lax.axis_size("dp")
    group_rows = tok * blk_count
    all_rows = group_rows * dp_count
    factor = 2.0 / math.sqrt(group_rows * all_rows)
    bits = dp_count.bit_length() - 1
    b = lax.axis_index("blk")
    y, c = b >> 1, b & 1
    place = b.astype(jnp.int32).reshape(1)
    k = CHUNKS
    part = tok // k

    rem = []
    for start, count in ((0, 1), (1, k - 1)):
        names = [("rows", j) for j in range(start, start + count)]
        out = run(
            functools.partial(fetch, [("arg", j * part, part, ("rows", j)) for _, j in names]),
            {"arg": fingerprints},
            {name: ((part, width), BF16) for name in names},
            {"sems": pltpu.SemaphoreType.DMA((count,))},
            limit=2 << 20,
        )
        rem += [blk_swap(out[name], 2) for name in names]
    sib = blk_swap(fingerprints, 1)
    rs = []

    base = {"place": place, "w_first": w_first, "w_second": w_second}
    out = run(
        first_stage,
        {**base, "own": fingerprints, "sib": sib},
        {
            "feats": ((2 * tok, width), BF16),
            "hidden": ((tok, hid), BF16),
            "gate": ((2, 256, tok), F32),
            "embed": ((2 * tok, emb), BF16),
            "sq": ((2 * tok, 128), F32),
            ("summed", 0): ((tok, emb), F32),
            "token": ((8, 128), F32),
        },
        {"acc": ((2 * tok, emb), F32)},
    )
    token = out["token"]
    hidden, gate, feats = [out["hidden"]], [out["gate"]], [out["feats"]]
    embed, sq, summed = [out["embed"]], [out["sq"]], [out["summed", 0]]
    for step in range(1, k + 1):
        last = step == k
        half = part // 2
        out = run(
            split,
            {"rem": rem[step - 1], "token": token},
            {("rows", h): ((half, width), BF16) for h in range(2)},
            {},
            limit=2 << 20,
        )
        ins = {**base, "rem": rem[step - 1]}
        for h in range(2):
            ins["rs", h] = blk_swap(out["rows", h], 1)
        for j in range(step):
            ins["feats", j] = feats[j]
            ins["embed", j] = embed[j]
            ins["sq", j] = sq[j]
            ins["summed", j] = summed[j]
        outs = {
            "feats": ((2 * part, width), BF16),
            "hidden": ((part, hid), BF16),
            "gate": ((2, 256, part), F32),
        }
        more = {
            "embed": ((2 * part, emb), BF16),
            "sq": ((2 * part, 128), F32),
            **{("summed", j): ((tok if j == 0 else part, emb), F32) for j in range(step + 1)},
        }
        scratch = {"acc": ((2 * part, emb), F32)}
        if last:
            for j in range(step):
                ins["hidden", j] = hidden[j]
                ins["gate", j] = gate[j]
            scratch = {**scratch, **more, "hidden": outs.pop("hidden"), "gate": outs.pop("gate")}
            scratch["sum_embed"] = ((2 * tok, emb), BF16)
            scratch["dembed"] = ((4, 2 * tok, emb // 4), BF16)
            for name in ("give", "keep"):
                outs[name] = ((256, 2 * tok), BF16)
                outs["second_" + name] = ((emb // 4, hid), F32)
            body = functools.partial(last_stage, factor)
        else:
            outs = {**outs, **more, "token": ((8, 128), F32)}
            body = functools.partial(next_stage, step)
        out = run(body, ins, outs, scratch)
        feats.append(out["feats"])
        if not last:
            hidden.append(out["hidden"])
            gate.append(out["gate"])
            token = out["token"]
            embed.append(out["embed"])
            sq.append(out["sq"])
            summed = [out["summed", j] for j in range(step + 1)]

    got = blk_swap(out["give"], 1)
    second_got = blk_swap(out["second_give"], 1)
    ins = {
        "keep": out["keep"],
        "got": got,
        "second_keep": out["second_keep"],
        "second_got": second_got,
    }
    for j in range(k + 1):
        ins["feats", j] = feats[j]
    rows_one, rows_two = CUT + 64 + 16, 256 - CUT + 16
    out = run(
        gradients,
        ins,
        {
            "one": ((8, rows_one, 256), F32),
            "two": ((8, rows_two, 256), F32),
            "kind_one": ((rows_one, 256), F32),
            "kind_two": ((rows_two, 256), F32),
        },
        {},
    )
    lanes = 256 * 8 // dp_count
    extra = dp_count // 8
    one = split_lanes(out["one"], (CUT, CUT + 64), extra)
    two = split_lanes(out["two"], (0, 0), extra)
    kind_one, kind_two = out["kind_one"][:, :lanes], out["kind_two"][:, :lanes]
    more = extra.bit_length() - 1
    shape = (2,) * more + (4, 2)
    shifts = [3 + more - 1 - n for n in range(more)] + [1, 0]
    zed, ex, rest = more, more + 1, list(range(more))
    one = Sum(one.reshape(shape + one.shape[1:]), kind_one, [ex, zed] + rest)
    two = Sum(two.reshape(shape + two.shape[1:]), kind_two, [zed] + rest + [ex])
    for step in range(more + 2):
        gots = lax.optimization_barrier((one.send(step, shifts), two.send(step, shifts)))
        one.receive(gots[0])
        two.receive(gots[1])

    packed = jnp.concatenate(
        [encode16(one.total, kind_one, one.tail), encode16(two.total, kind_two, two.tail)], 0
    )
    across = blk_swap(packed, 2)
    pair = jnp.stack([packed, across])
    beside = blk_swap(pair, 1)
    here = halves(jnp.stack([packed, beside[0]]), 0, c)
    there = halves(jnp.stack([across, beside[1]]), 0, c)
    low = [jnp.where(y == 0, h, t) for h, t in zip(here, there)]
    high = [jnp.where(y == 0, t, h) for h, t in zip(here, there)]
    every = jnp.stack(low + high)
    one = decode16(every[:, :rows_one], kind_one, one.tail)
    two = decode16(every[:, rows_one:], kind_two, two.tail)
    first = jnp.concatenate([one[:, :CUT], two[:, : 256 - CUT]], 1).reshape(hid, lanes)
    second = one[:, CUT : CUT + 64]
    second = jnp.concatenate([second[..., : lanes // 2], second[..., lanes // 2 :]], 1)
    return first.T, second.reshape(emb, lanes // 2).T


def solution(mesh):
    in_specs = (P(("blk", "dp"), None), P(), P())
    out_specs = (P("dp", None), P("dp", None))
    return jax.shard_map(
        per_device, mesh=mesh, in_specs=in_specs, out_specs=out_specs, check_vma=False
    )
```

```python
import functools
import math

import jax
import jax.numpy as jnp
from jax import lax
from jax.experimental import pallas as pl
from jax.experimental.pallas import tpu as pltpu
from jax.sharding import PartitionSpec as P

F32 = jnp.float32
BF16 = jnp.bfloat16
F16 = jnp.float16
NN = (((1,), (0,)), ((), ()))
NT = (((1,), (1,)), ((), ()))
TN = (((0,), (0,)), ((), ()))
CHUNKS = 3
CUT = 144
VMEM_LIMIT = 20 * 1024 * 1024


def dot(left, right, dims=NN):
    return lax.dot_general(left, right, dims, preferred_element_type=F32)


def blk_swap(value, bit):
    count = lax.axis_size("blk")
    return lax.ppermute(value, "blk", [(b, b ^ bit) for b in range(count)])


def dp_swap(value, bit):
    count = lax.axis_size("dp")
    return lax.ppermute(value, "dp", [(d, d ^ bit) for d in range(count)])


def quarter_of(place, j):
    return pl.multiple_of((place ^ j) * 256, 256)


def encode(place, feats, kept, w_first, w_second, hidden_out, gate_out, acc):
    for j in range(4):
        units = pl.ds(quarter_of(place, j), 256)
        pre = dot(feats[...], w_first[:, units])
        sig = jax.nn.sigmoid(pre)
        hidden = (pre * sig).astype(BF16)
        hidden_out[:, j * 256 : (j + 1) * 256] = hidden[:kept]
        if j < 2:
            gate = sig[:kept] * (1.0 + pre[:kept] * (1.0 - sig[:kept]))
            gate_out[j] = gate.T
        part = dot(hidden, w_second[units, :])
        if j == 0:
            acc[...] = part
        else:
            acc[...] += part
    return acc[...].astype(BF16)


def residual(inter, pred, sq_rows, sq_cols, emb):
    tanimoto = inter / (sq_rows + sq_cols - inter)
    return (pred * (1.0 / math.sqrt(emb)) - tanimoto).astype(BF16)


def first_stage(i, o, s):
    tok, emb = i["own"].shape[0], i["w_second"].shape[1]
    feats = o["feats"]
    feats[:tok] = i["own"][...]
    feats[tok:] = i["sib"][...]
    embed = encode(
        lax.axis_index("blk"), feats, tok, i["w_first"], i["w_second"], o["hidden"], o["gate"], s["acc"]
    )
    o["embed"][...] = embed
    wide = feats[...].astype(F32)
    sq = jnp.broadcast_to(jnp.sum(wide * wide, axis=1, keepdims=True), o["sq"].shape)
    o["sq"][...] = sq
    sq_cols = sq.T[:1]
    inter = dot(feats[:tok], feats[...], NT)
    pred = dot(embed[:tok], embed, NT)
    resid = residual(inter, pred, sq[:tok, :1], sq_cols, emb)
    o["summed", 0][...] = dot(resid, embed)
    o["token"][...] = jnp.zeros((8, 128), F32)


def add_columns(k, feats, embed, sq, embed_new, summed, emb, tok, part):
    top = feats[k][...]
    inter = dot(top, top, NT)
    at = lax.broadcasted_iota(jnp.int32, inter.shape, 0)
    to = lax.broadcasted_iota(jnp.int32, inter.shape, 1)
    diagonal = jnp.where(at == to, inter, 0.0)
    sq_rows = jnp.sum(diagonal, axis=1, keepdims=True)
    sq_cols = jnp.sum(diagonal, axis=0, keepdims=True)
    sq[k][...] = jnp.broadcast_to(sq_rows, sq[k].shape)
    resid = residual(inter, dot(embed_new, embed_new, NT), sq_rows, sq_cols, emb)
    total = dot(resid[:, :part], embed_new, TN)
    for j in range(k):
        pieces = [(0, tok, True), (tok, tok, False)] if j == 0 else [(0, 2 * part, True)]
        for start, count, keep in pieces:
            rows = pl.ds(start, count)
            old_embed = embed[j][rows, :]
            inter = dot(feats[j][rows, :], top, NT)
            pred = dot(old_embed, embed_new, NT)
            resid = residual(inter, pred, sq[j][rows, :1], sq_cols, emb)
            if keep:
                mine = resid if j == 0 else resid[:part]
                summed[j][...] += dot(mine, embed_new)
            total += dot(resid[:, :part], old_embed, TN)
    return total


def next_stage(k, i, o, s):
    tok, part, emb = i["summed", 0].shape[0], i["rem"].shape[0], i["w_second"].shape[1]
    feats = [i["feats", j] for j in range(k)] + [o["feats"]]
    feats[k][:part] = i["rem"][...]
    half = part // 2
    feats[k][part : part + half] = i["rs", 0][...]
    feats[k][part + half :] = i["rs", 1][...]
    embed = [i["embed", j] for j in range(k)]
    sq = [i["sq", j] for j in range(k)] + [o["sq"]]
    embed_new = encode(
        lax.axis_index("blk"), feats[k], part, i["w_first"], i["w_second"], o["hidden"], o["gate"], s["acc"]
    )
    o["embed"][...] = embed_new
    summed = [o["summed", j] for j in range(k + 1)]
    for j in range(k):
        summed[j][...] = i["summed", j][...]
    summed[k][...] = add_columns(k, feats, embed, sq, embed_new, summed, emb, tok, part)
    if "token" in o:
        o["token"][...] = jnp.zeros((8, 128), F32)


def last_stage(factor, i, o, s):
    k = CHUNKS
    place = lax.axis_index("blk")
    next_stage(k, i, {**s, **o}, s)
    tok, part = i["summed", 0].shape[0], i["rem"].shape[0]
    wide = i["w_second"].shape[1] // 4
    starts = [0] + [tok + part * j for j in range(k)]
    sizes = [tok] + [part] * k
    for j in range(k + 1):
        rows = pl.ds(starts[j], sizes[j])
        piece = (s["summed", j][...] * factor).astype(BF16)
        s["sum_embed"][rows, :] = piece
        for q in range(4):
            s["dembed"][q, rows, :] = piece[:, q * wide : (q + 1) * wide]
    gates = [i["gate", j] for j in range(k)] + [s["gate"]]
    hiddens = [i["hidden", j] for j in range(k)] + [s["hidden"]]
    for n, name in ((1, "give"), (0, "keep")):
        units = pl.ds(quarter_of(place, n), 256)
        turned = dot(i["w_second"][units, :], s["sum_embed"][...], NT)
        for j in range(k + 1):
            rows = slice(starts[j], starts[j] + sizes[j])
            o[name][:, rows] = (turned[:, rows] * gates[j][n]).astype(BF16)
        second_share(place, place ^ n, s["dembed"], hiddens, o["second_" + name])


def second_share(place, quarter, dembed, hiddens, out):
    total, start = None, 0
    for hidden in hiddens:
        count = hidden.shape[0]
        part = dot(dembed[quarter, start : start + count, :], hidden[...], TN)
        total = part if total is None else total + part
        start += count
    for j in range(4):
        out[:, pl.ds(quarter_of(place, j), 256)] = total[:, j * 256 : (j + 1) * 256]


def exponent(bound):
    return jnp.clip(jnp.ceil(jnp.log2(jnp.maximum(bound, 1e-30))) + 1.0, -100.0, 120.0)


def gradients(i, o, s):
    second = i["second_keep"][...] + i["second_got"][...]
    sums = jnp.sum(jnp.abs(i["keep"][...].astype(F32)), axis=1, keepdims=True)
    sums += jnp.sum(jnp.abs(i["got"][...].astype(F32)), axis=1, keepdims=True)
    exp_first = exponent(3.0 * jnp.max(sums, axis=0, keepdims=True))
    most = jnp.max(jnp.abs(second), axis=1, keepdims=True)
    exp_second = exponent(jnp.max(most, axis=0, keepdims=True))
    exp_first = jnp.broadcast_to(exp_first, (8, 256))
    exp_second = jnp.broadcast_to(exp_second, (8, 256))
    one, two = o["one"], o["two"]
    top, bottom = CUT, 256 - CUT
    s["second"][...] = second
    me = lax.axis_index("dp") // (lax.axis_size("dp") // 8)
    for d in range(8):
        block = s["second"][:, pl.ds(pl.multiple_of((me ^ d) * 128, 128), 128)]
        one[d, top : top + 64, :128] = block[:64]
        one[d, top : top + 64, 128:] = block[64:]
        one[d, top + 64 : top + 72] = exp_first
        one[d, top + 72 :] = exp_second
        two[d, bottom : bottom + 8] = exp_first
        two[d, bottom + 8 :] = exp_first
    o["kind_one"][:top] = jnp.zeros((top, 256), F32)
    o["kind_one"][top : top + 64] = jnp.ones((64, 256), F32)
    o["kind_one"][top + 64 :] = jnp.full((16, 256), 2.0, F32)
    o["kind_two"][:bottom] = jnp.zeros((bottom, 256), F32)
    o["kind_two"][bottom:] = jnp.full((16, 256), 2.0, F32)
    for d in range(8):
        block, at = None, 0
        lanes = pl.ds(pl.multiple_of((me ^ d) * 256, 256), 256)
        for j in range(CHUNKS + 1):
            f = i["feats", j]
            count = f.shape[0] // 2
            for half, name in enumerate(("keep", "got")):
                rows = f[half * count : (half + 1) * count, lanes]
                piece = dot(i[name][:, at : at + count], rows)
                block = piece if block is None else block + piece
            at += count
        one[d, :top] = block[:top]
        two[d, :bottom] = block[top:]


def run(body, ins, outs, scratch, limit=VMEM_LIMIT):
    names_in, names_out, names_s = list(ins), list(outs), list(scratch)

    def kernel(*refs):
        n, m = len(names_in), len(names_out)
        i = dict(zip(names_in, refs[:n]))
        o = dict(zip(names_out, refs[n : n + m]))
        body(i, o, dict(zip(names_s, refs[n + m :])))

    vmem = pltpu.VMEM
    spaces = {"arg": pl.ANY}
    shapes = [jax.ShapeDtypeStruct(*v) for v in outs.values()]
    got = pl.pallas_call(
        kernel,
        out_shape=shapes,
        in_specs=[pl.BlockSpec(memory_space=spaces.get(n, vmem)) for n in names_in],
        out_specs=[pl.BlockSpec(memory_space=vmem)] * len(shapes),
        scratch_shapes=[vmem(*v) if isinstance(v, tuple) else v for v in scratch.values()],
        compiler_params=pltpu.CompilerParams(vmem_limit_bytes=limit),
        cost_estimate=pl.CostEstimate(flops=1, bytes_accessed=1, transcendentals=0),
    )(*ins.values())
    return dict(zip(names_out, got))


def split(i, o, s):
    half = i["rem"].shape[0] // 2
    for h in range(2):
        o["rows", h][...] = i["rem"][h * half : (h + 1) * half]


def fetch(pairs, i, o, s):
    copies = []
    for n, (source, start, count, target) in enumerate(pairs):
        rows = i[source].at[pl.ds(start, count), :]
        copies.append(pltpu.make_async_copy(rows, o[target], s["sems"].at[n]))
        copies[-1].start()
    for copy in copies:
        copy.wait()


def place_quarters(i, o, s):
    me = lax.axis_index("blk")
    for j in range(4):
        q = me ^ j
        first = jnp.concatenate([i["one"][j, :CUT], i["two"][j, : 256 - CUT]], 0)
        o["first"][:, pl.ds(pl.multiple_of(q * 256, 256), 256)] = first.T
        block = i["one"][j, CUT : CUT + 64]
        second = jnp.concatenate([block[:, :128], block[:, 128:]], 0)
        o["second"][:, pl.ds(pl.multiple_of(q * 128, 128), 128)] = second.T


def encode16(total, kind, tail):
    first, second = exps_of(total, tail)
    e = jnp.where(kind == 0.0, first, second)
    scale = jnp.where(kind == 2.0, 1.0, jnp.exp2(15.0 - e))
    return (total * scale).astype(F16)


def decode16(got, kind, tail):
    got = got.astype(F32)
    first, second = exps_of(got, tail)
    e = jnp.where(kind == 0.0, first, second)
    return got * jnp.where(kind == 2.0, 1.0, jnp.exp2(e - 15.0))


def exps_of(value, tail):
    rows = value.ndim - 2
    return [lax.slice_in_dim(value, tail + at, tail + at + 1, axis=rows) for at in (0, 8)]


def halves(value, axis, mine):
    low = lax.index_in_dim(value, 0, axis, keepdims=False)
    high = lax.index_in_dim(value, 1, axis, keepdims=False)
    return jnp.where(mine == 0, low, high), jnp.where(mine == 0, high, low)


def pick(total, axis, index):
    if isinstance(index, int):
        return lax.index_in_dim(total, index, axis, keepdims=False)
    return lax.dynamic_index_in_dim(total, index, axis, keepdims=False)


class Sum:
    def __init__(self, total, kind, order, relative):
        self.total, self.kind = total, kind
        self.tail = total.shape[-2] - 16
        self.axes = list(range(total.ndim - 2))
        self.order, self.relative = order, relative

    def send(self, step, shifts):
        axis = self.order[step]
        at = self.axes.index(axis)
        size = self.total.shape[at]
        me = 0
        if axis >= self.relative:
            me = (lax.axis_index("dp") >> shifts[axis]) & (size - 1)
        gots = []
        for o in range(size - 1, 0, -1):
            give = pick(self.total, at, me ^ o)
            gots.append(dp_swap(encode16(give, self.kind, self.tail), o << shifts[axis]))
        self.axes.pop(at)
        self.keep = pick(self.total, at, me)
        return gots

    def receive(self, gots):
        others = [decode16(g, self.kind, self.tail) for g in gots]
        total, top = self.keep, self.keep
        for other in others:
            total = total + other
            top = jnp.maximum(top, other)
        self.total = jnp.where(self.kind == 2.0, top + float(len(others)), total)


def split_lanes(packed, bounds, count):
    if count == 1:
        return packed
    blocks, rows, lanes = packed.shape
    plain = packed.reshape(blocks, rows, count, lanes // count)
    paired = packed.reshape(blocks, rows, 2, count, lanes // 2 // count)
    plain = jnp.moveaxis(plain, 2, 1)
    paired = jnp.moveaxis(paired, 3, 1).reshape(plain.shape)
    row = lax.broadcasted_iota(jnp.int32, plain.shape, 2)
    both = jnp.where((row >= bounds[0]) & (row < bounds[1]), paired, plain)
    return both.reshape(blocks * count, rows, lanes // count)


def per_device(fingerprints, w_first, w_second):
    tok, width = fingerprints.shape
    hid, emb = w_second.shape
    blk_count = lax.axis_size("blk")
    dp_count = lax.axis_size("dp")
    group_rows = tok * blk_count
    all_rows = group_rows * dp_count
    factor = 2.0 / math.sqrt(group_rows * all_rows)
    bits = dp_count.bit_length() - 1
    k = CHUNKS
    part = tok // k

    rem = []
    rem.append(blk_swap(fingerprints[:part], 2))
    for start, count in ((1, k - 1),):
        names = [("rows", j) for j in range(start, start + count)]
        out = run(
            functools.partial(fetch, [("arg", j * part, part, ("rows", j)) for _, j in names]),
            {"arg": fingerprints},
            {name: ((part, width), BF16) for name in names},
            {"sems": pltpu.SemaphoreType.DMA((count,))},
            limit=2 << 20,
        )
        rem += [blk_swap(out[name], 2) for name in names]
    sib = blk_swap(fingerprints, 1)
    rs = []

    base = {"w_first": w_first, "w_second": w_second}
    out = run(
        first_stage,
        {**base, "own": fingerprints, "sib": sib},
        {
            "feats": ((2 * tok, width), BF16),
            "hidden": ((tok, hid), BF16),
            "gate": ((2, 256, tok), F32),
            "embed": ((2 * tok, emb), BF16),
            "sq": ((2 * tok, 128), F32),
            ("summed", 0): ((tok, emb), F32),
            "token": ((8, 128), F32),
        },
        {"acc": ((2 * tok, emb), F32)},
    )
    token = out["token"]
    hidden, gate, feats = [out["hidden"]], [out["gate"]], [out["feats"]]
    embed, sq, summed = [out["embed"]], [out["sq"]], [out["summed", 0]]
    for step in range(1, k + 1):
        last = step == k
        half = part // 2
        out = run(
            split,
            {"rem": rem[step - 1], "token": token},
            {("rows", h): ((half, width), BF16) for h in range(2)},
            {},
            limit=2 << 20,
        )
        ins = {**base, "rem": rem[step - 1]}
        for h in range(2):
            ins["rs", h] = blk_swap(out["rows", h], 1)
        for j in range(step):
            ins["feats", j] = feats[j]
            ins["embed", j] = embed[j]
            ins["sq", j] = sq[j]
            ins["summed", j] = summed[j]
        outs = {
            "feats": ((2 * part, width), BF16),
            "hidden": ((part, hid), BF16),
            "gate": ((2, 256, part), F32),
        }
        more = {
            "embed": ((2 * part, emb), BF16),
            "sq": ((2 * part, 128), F32),
            **{("summed", j): ((tok if j == 0 else part, emb), F32) for j in range(step + 1)},
        }
        scratch = {"acc": ((2 * part, emb), F32)}
        if last:
            for j in range(step):
                ins["hidden", j] = hidden[j]
                ins["gate", j] = gate[j]
            scratch = {**scratch, **more, "hidden": outs.pop("hidden"), "gate": outs.pop("gate")}
            scratch["sum_embed"] = ((2 * tok, emb), BF16)
            scratch["dembed"] = ((4, 2 * tok, emb // 4), BF16)
            for name in ("give", "keep"):
                outs[name] = ((256, 2 * tok), BF16)
                outs["second_" + name] = ((emb // 4, hid), F32)
            body = functools.partial(last_stage, factor)
        else:
            outs = {**outs, **more, "token": ((8, 128), F32)}
            body = functools.partial(next_stage, step)
        out = run(body, ins, outs, scratch)
        feats.append(out["feats"])
        if not last:
            hidden.append(out["hidden"])
            gate.append(out["gate"])
            token = out["token"]
            embed.append(out["embed"])
            sq.append(out["sq"])
            summed = [out["summed", j] for j in range(step + 1)]

    got = blk_swap(out["give"], 1)
    second_got = blk_swap(out["second_give"], 1)
    ins = {
        "keep": out["keep"],
        "got": got,
        "second_keep": out["second_keep"],
        "second_got": second_got,
    }
    for j in range(k + 1):
        ins["feats", j] = feats[j]
    rows_one, rows_two = CUT + 64 + 16, 256 - CUT + 16
    out = run(
        gradients,
        ins,
        {
            "one": ((8, rows_one, 256), F32),
            "two": ((8, rows_two, 256), F32),
            "kind_one": ((rows_one, 256), F32),
            "kind_two": ((rows_two, 256), F32),
        },
        {"second": ((emb // 4, hid), F32)},
    )
    lanes = 256 * 8 // dp_count
    extra = dp_count // 8
    one = split_lanes(out["one"], (CUT, CUT + 64), extra)
    two = split_lanes(out["two"], (0, 0), extra)
    kind_one, kind_two = out["kind_one"][:, :lanes], out["kind_two"][:, :lanes]
    more = extra.bit_length() - 1
    shape = (4, 2) + (2,) * more
    shifts = [more + 1, more] + [more - 1 - n for n in range(more)]
    rest = list(range(2, more + 2))
    one = Sum(one.reshape(shape + one.shape[1:]), kind_one, [1, 0] + rest, 2)
    two = Sum(two.reshape(shape + two.shape[1:]), kind_two, [0] + rest + [1], 2)
    for step in range(more + 2):
        gots = lax.optimization_barrier((one.send(step, shifts), two.send(step, shifts)))
        one.receive(gots[0])
        two.receive(gots[1])

    packed = jnp.concatenate(
        [encode16(one.total, kind_one, one.tail), encode16(two.total, kind_two, two.tail)], 0
    )
    across = blk_swap(packed, 2)
    pair = jnp.stack([packed, across])
    beside = blk_swap(pair, 1)
    every = jnp.stack([packed, beside[0], across, beside[1]])
    one = decode16(every[:, :rows_one], kind_one, one.tail)
    two = decode16(every[:, rows_one:], kind_two, two.tail)
    if extra == 1:
        out = run(
            place_quarters,
            {"one": one, "two": two},
            {"first": ((lanes, hid), F32), "second": ((lanes // 2, emb), F32)},
            {},
        )
        return out["first"], out["second"]
    b = lax.axis_index("blk")
    order = jnp.arange(4) ^ b
    first = jnp.concatenate([one[:, :CUT], two[:, : 256 - CUT]], 1)[order].reshape(hid, lanes)
    second = one[order, CUT : CUT + 64]
    second = jnp.concatenate([second[..., : lanes // 2], second[..., lanes // 2 :]], 1)
    return first.T, second.reshape(emb, lanes // 2).T


def solution(mesh):
    in_specs = (P(("blk", "dp"), None), P(), P())
    out_specs = (P("dp", None), P("dp", None))
    return jax.shard_map(
        per_device, mesh=mesh, in_specs=in_specs, out_specs=out_specs, check_vma=False
    )
```

```python
import functools
import math

import jax
import jax.numpy as jnp
from jax import lax
from jax.experimental import pallas as pl
from jax.experimental.pallas import tpu as pltpu
from jax.sharding import PartitionSpec as P

F32 = jnp.float32
BF16 = jnp.bfloat16
F16 = jnp.float16
NN = (((1,), (0,)), ((), ()))
NT = (((1,), (1,)), ((), ()))
TN = (((0,), (0,)), ((), ()))
CHUNKS = 3
CUT = 176
VMEM_LIMIT = 20 * 1024 * 1024


def dot(left, right, dims=NN):
    return lax.dot_general(left, right, dims, preferred_element_type=F32)


def blk_swap(value, bit):
    count = lax.axis_size("blk")
    return lax.ppermute(value, "blk", [(b, b ^ bit) for b in range(count)])


def dp_swap(value, bit):
    count = lax.axis_size("dp")
    return lax.ppermute(value, "dp", [(d, d ^ bit) for d in range(count)])


def quarter_of(place, j):
    return pl.multiple_of((place ^ j) * 256, 256)


def encode(feats, w_first, w_second, pre_out=None, hidden_out=None):
    pre = dot(feats, w_first[...])
    hidden = (pre * jax.nn.sigmoid(pre)).astype(BF16)
    if pre_out is not None:
        pre_out[...] = pre
        hidden_out[...] = hidden
    return dot(hidden, w_second[...]).astype(BF16)


def put_gates(place, pre, out):
    for n in range(2):
        quarter = pre[:, pl.ds(quarter_of(place, n), 256)]
        sig = jax.nn.sigmoid(quarter)
        out[n] = (sig * (1.0 + quarter * (1.0 - sig))).T


def residual(inter, pred, sq_rows, sq_cols, emb):
    tanimoto = inter / (sq_rows + sq_cols - inter)
    return (pred * (1.0 / math.sqrt(emb)) - tanimoto).astype(BF16)


def first_stage(i, o, s):
    tok, emb = i["own"].shape[0], i["w_second"].shape[1]
    feats = o["feats"]
    feats[:tok] = i["own"][...]
    feats[tok:] = i["sib"][...]
    step = tok // 3
    for r in range(0, tok, step):
        rows = slice(r, r + step)
        embed = encode(feats[rows, :], i["w_first"], i["w_second"], s["pre"], s["hidden"])
        o["embed"][rows, :] = embed
        o["hidden"][rows, :] = s["hidden"][...]
        for n in range(2):
            quarter = s["pre"][:, pl.ds(quarter_of(lax.axis_index("blk"), n), 256)]
            sig = jax.nn.sigmoid(quarter)
            o["gate"][n, :, rows] = (sig * (1.0 + quarter * (1.0 - sig))).T
    for r in range(tok, 2 * tok, step):
        rows = slice(r, r + step)
        o["embed"][rows, :] = encode(feats[rows, :], i["w_first"], i["w_second"])
    embed = o["embed"][...]
    wide = feats[...].astype(F32)
    sq = jnp.broadcast_to(jnp.sum(wide * wide, axis=1, keepdims=True), o["sq"].shape)
    o["sq"][...] = sq
    sq_cols = sq.T[:1]
    inter = dot(feats[:tok], feats[...], NT)
    pred = dot(embed[:tok], embed, NT)
    resid = residual(inter, pred, sq[:tok, :1], sq_cols, emb)
    o["summed", 0][...] = dot(resid, embed)
    o["token"][...] = jnp.zeros((8, 128), F32)


def diagonals(square):
    at = lax.broadcasted_iota(jnp.int32, square.shape, 0)
    to = lax.broadcasted_iota(jnp.int32, square.shape, 1)
    only = jnp.where(at == to, square, 0.0)
    return jnp.sum(only, axis=1, keepdims=True), jnp.sum(only, axis=0, keepdims=True)


def rem_stage(k, i, o, s):
    emb = i["w_second"].shape[1]
    top = i["new"][...]
    embed_new = encode(top, i["w_first"], i["w_second"], s["pre"], o["hidden"])
    put_gates(lax.axis_index("blk"), s["pre"], o["gate"])
    o["embed"][...] = embed_new
    _, sq_cols = diagonals(dot(top, top, NT))
    tok = i["feats", 0].shape[0] // 2
    total = None
    for name in [0] + [("rs", j) for j in range(1, k)]:
        rows = pl.ds(tok, tok) if name == 0 else pl.ds(0, top.shape[0])
        old = i["embed", name][rows, :]
        inter = dot(i["feats", name][rows, :], top, NT)
        resid = residual(inter, dot(old, embed_new, NT), i["sq", name][rows, :1], sq_cols, emb)
        part = dot(resid, old, TN)
        total = part if total is None else total + part
    o["total"][...] = total


def rs_stage(k, i, o, s):
    emb = i["w_second"].shape[1]
    half = i["new", 0].shape[0]
    part = 2 * half
    for h in range(2):
        o["feats"][h * half : (h + 1) * half] = i["new", h][...]
    embed_rs = encode(o["feats"][...], i["w_first"], i["w_second"])
    s["both"][:part] = i["feats", ("rem", k)][...]
    s["both"][part:] = o["feats"][...]
    s["embeds"][:part] = i["embed", ("rem", k)][...]
    s["embeds"][part:] = embed_rs
    top, embed_new = s["both"][...], s["embeds"][...]
    inter = dot(top, top, NT)
    sq_rows, sq_cols = diagonals(inter)
    if "embed" in o:
        o["embed"][...] = embed_rs
        o["sq_rem"][...] = jnp.broadcast_to(sq_rows[:part], o["sq_rem"].shape)
        o["sq_rs"][...] = jnp.broadcast_to(sq_rows[part:], o["sq_rs"].shape)
        o["token"][...] = jnp.zeros((8, 128), F32)
    pred = dot(embed_new[:part], embed_new, NT)
    resid = residual(inter[:part], pred, sq_rows[:part], sq_cols, emb)
    total = i["total"][...] + dot(resid, embed_new)
    out = []
    for j in range(k):
        name = ("rem", j) if j else 0
        rows = pl.ds(0, i["summed", j].shape[0])
        old = i["embed", name][rows, :]
        inter = dot(i["feats", name][rows, :], top, NT)
        pred = dot(old, embed_new, NT)
        resid = residual(inter, pred, i["sq", name][rows, :1], sq_cols, emb)
        total += dot(resid[:, :part], old, TN)
        out.append(i["summed", j][...] + dot(resid, embed_new))
    out.append(total)
    for j in range(k + 1):
        if ("summed", j) in o:
            o["summed", j][...] = out[j]
    return out


def last_stage(factor, i, o, s):
    place = lax.axis_index("blk")
    wide = i["w_second"].shape[1] // 4
    start = 0
    for value in rs_stage(CHUNKS, i, o, s):
        rows = pl.ds(start, value.shape[0])
        piece = (value * factor).astype(BF16)
        o["dembed"][rows, :] = piece
        for q in range(4):
            o["quarters"][q, rows, :] = piece[:, q * wide : (q + 1) * wide]
        start += value.shape[0]
    dpre_share(place, 1, i, o["dembed"], o["give"])
    second_share(place ^ 1, o["quarters"], hiddens_of(i), o["second_give"])


def hiddens_of(i):
    return [i["hidden", j] for j in range(CHUNKS + 1)]


def dpre_share(place, n, i, dembed, out):
    turned = dot(i["w_second"][pl.ds(quarter_of(place, n), 256), :], dembed[...], NT)
    start = 0
    for j in range(CHUNKS + 1):
        gate = i["gate", j][n]
        rows = slice(start, start + gate.shape[1])
        out[:, rows] = (turned[:, rows] * gate).astype(BF16)
        start = rows.stop


def own_share(i, o, s):
    place = lax.axis_index("blk")
    dpre_share(place, 0, i, i["dembed"], o["keep"])
    second_share(place, i["quarters"], hiddens_of(i), o["second"])
    me = dp_high()
    for d in range(8):
        o["first"][d] = first_block(o["keep"], core_rows(i, 0), me ^ d)


def dp_high():
    return lax.axis_index("dp") // (lax.axis_size("dp") // 8)


def core_rows(i, core):
    both = i["feats", 0]
    tok = both.shape[0] // 2
    name = ("rem", "rs")[core]
    return [(both, core * tok, tok)] + [
        (i["feats", (name, j)], 0, i["feats", (name, j)].shape[0]) for j in range(1, CHUNKS + 1)
    ]


def first_block(dpre, rows, block, top=0, bottom=256):
    lanes = pl.ds(pl.multiple_of(block * 256, 256), 256)
    total, at = None, 0
    for ref, start, count in rows:
        piece = dot(dpre[top:bottom, at : at + count], ref[pl.ds(start, count), lanes])
        total = piece if total is None else total + piece
        at += count
    return total


def second_share(quarter, dembed, hiddens, out):
    total, start = None, 0
    for hidden in hiddens:
        count = hidden.shape[0]
        part = dot(dembed[quarter, start : start + count, :], hidden[...], TN)
        total = part if total is None else total + part
        start += count
    out[...] = total


def exponent(bound):
    return jnp.clip(jnp.ceil(jnp.log2(jnp.maximum(bound, 1e-30))) + 1.0, -100.0, 120.0)


def put_tail(ref, d, start, exp_first, exp_second):
    ref[d, start : start + 8] = exp_first
    ref[d, start + 8 : start + 16] = exp_second


def put_second(ref, d, second, block):
    value = second[:, pl.ds(pl.multiple_of(block * 128, 128), 128)]
    ref[d, CUT : CUT + 64, :128] = value[:64]
    ref[d, CUT : CUT + 64, 128:] = value[64:]


def first_gradients(i, o, s):
    o["second"][...] = i["second_keep"][...] + i["second_got"][...]
    sums = jnp.sum(jnp.abs(i["keep"][...].astype(F32)), axis=1, keepdims=True)
    sums += jnp.sum(jnp.abs(i["got"][...].astype(F32)), axis=1, keepdims=True)
    exp_first = exponent(3.0 * jnp.max(sums, axis=0, keepdims=True))
    most = jnp.max(jnp.abs(o["second"][...]), axis=1, keepdims=True)
    exp_second = exponent(jnp.max(most, axis=0, keepdims=True))
    o["exps"][0] = jnp.broadcast_to(exp_first, (8, 256))
    o["exps"][1] = jnp.broadcast_to(exp_second, (8, 256))
    bottom = 256 - CUT
    o["kind_one"][:CUT] = jnp.zeros((CUT, 256), F32)
    o["kind_one"][CUT : CUT + 64] = jnp.ones((64, 256), F32)
    o["kind_one"][CUT + 64 :] = jnp.full((16, 256), 2.0, F32)
    o["kind_two"][:bottom] = jnp.zeros((bottom, 256), F32)
    o["kind_two"][bottom:] = jnp.full((16, 256), 2.0, F32)
    o["kind_all"][:256] = jnp.zeros((256, 256), F32)
    o["kind_all"][256:320] = jnp.ones((64, 256), F32)
    o["kind_all"][320:] = jnp.full((16, 256), 2.0, F32)
    me = dp_high()
    for z in range(4):
        d = 2 * z + 1
        value = first_block(i["got"], core_rows(i, 1), me ^ d, 0, CUT)
        o["one"][z, :CUT] = value + i["first"][d, :CUT]
        put_second(o["one"], z, o["second"], me ^ d)
        put_tail(o["one"], z, CUT + 64, o["exps"][0], o["exps"][1])


def other_gradients(i, o, s):
    me = dp_high()
    rows = core_rows(i, 1)
    bottom = 256 - CUT
    for z in range(4):
        for x in range(2):
            d = 2 * z + x
            top = CUT if x else 0
            value = first_block(i["got"], rows, me ^ d, top, 256) + i["first"][d, top:]
            o["two"][d, :bottom] = value[CUT - top :]
            put_tail(o["two"], d, bottom, i["exps"][0], i["exps"][0])
            if x == 0:
                o["one"][z, :CUT] = value[:CUT]
                put_second(o["one"], z, i["second"], me ^ d)
                put_tail(o["one"], z, CUT + 64, i["exps"][0], i["exps"][1])


def run(body, ins, outs, scratch, limit=VMEM_LIMIT):
    names_in, names_out, names_s = list(ins), list(outs), list(scratch)

    def kernel(*refs):
        n, m = len(names_in), len(names_out)
        i = dict(zip(names_in, refs[:n]))
        o = dict(zip(names_out, refs[n : n + m]))
        body(i, o, dict(zip(names_s, refs[n + m :])))

    vmem = pltpu.VMEM
    spaces = {"arg": pl.ANY}
    shapes = [jax.ShapeDtypeStruct(*v) for v in outs.values()]
    got = pl.pallas_call(
        kernel,
        out_shape=shapes,
        in_specs=[pl.BlockSpec(memory_space=spaces.get(n, vmem)) for n in names_in],
        out_specs=[pl.BlockSpec(memory_space=vmem)] * len(shapes),
        scratch_shapes=[vmem(*v) if isinstance(v, tuple) else v for v in scratch.values()],
        compiler_params=pltpu.CompilerParams(vmem_limit_bytes=limit),
        cost_estimate=pl.CostEstimate(flops=1, bytes_accessed=1, transcendentals=0),
    )(*ins.values())
    return dict(zip(names_out, got))


def split(i, o, s):
    half = i["rem"].shape[0] // 2
    for h in range(2):
        o["rows", h][...] = i["rem"][h * half : (h + 1) * half]


def fetch(pairs, i, o, s):
    copies = []
    for n, (source, start, count, target) in enumerate(pairs):
        rows = i[source].at[pl.ds(start, count), :]
        copies.append(pltpu.make_async_copy(rows, o[target], s["sems"].at[n]))
        copies[-1].start()
    for copy in copies:
        copy.wait()


def turn_quarter(i, o, s):
    one, two, out = i["one"], i["two"], o["all"]
    bottom = 256 - CUT
    out[:256] = jnp.concatenate([one[:CUT], two[:bottom]], 0).T
    block = one[CUT : CUT + 64]
    second = jnp.concatenate([block[:, :128], block[:, 128:]], 0).T
    out[256:320, :128] = second[:64]
    out[256:320, 128:] = second[64:]
    out[320:328, :128] = one[CUT + 64 : CUT + 72, :128]
    lane = lax.broadcasted_iota(jnp.int32, (8, 128), 1)
    tail = two[bottom : bottom + 8, 128:]
    out[320:328, 128:] = jnp.where(lane < CUT - 128, one[CUT + 64 : CUT + 72, 128:], tail)
    out[328:] = one[CUT + 72 :]


def place_quarters(i, o, s):
    me = lax.axis_index("blk")
    for j in range(4):
        q = me ^ j
        o["first"][:, pl.ds(pl.multiple_of(q * 256, 256), 256)] = i["all"][j, :256]
        columns = pl.ds(pl.multiple_of(q * 128, 128), 128)
        o["second"][:64, columns] = i["all"][j, 256:320, :128]
        o["second"][64:, columns] = i["all"][j, 256:320, 128:]


def encode16(total, kind, tail):
    first, second = [jnp.exp2(15.0 - e) for e in exps_of(total, tail)]
    scale = jnp.where(kind == 0.0, first, jnp.where(kind == 1.0, second, 1.0))
    return (total * scale).astype(F16)


def decode16(got, kind, tail):
    got = got.astype(F32)
    first, second = [jnp.exp2(e - 15.0) for e in exps_of(got, tail)]
    return got * jnp.where(kind == 0.0, first, jnp.where(kind == 1.0, second, 1.0))


def exps_of(value, tail):
    rows = value.ndim - 2
    return [lax.slice_in_dim(value, tail + at, tail + at + 1, axis=rows) for at in (0, 8)]


def halves(value, axis, mine):
    low = lax.index_in_dim(value, 0, axis, keepdims=False)
    high = lax.index_in_dim(value, 1, axis, keepdims=False)
    return jnp.where(mine == 0, low, high), jnp.where(mine == 0, high, low)


def pick(total, axis, index):
    if isinstance(index, int):
        return lax.index_in_dim(total, index, axis, keepdims=False)
    return lax.dynamic_index_in_dim(total, index, axis, keepdims=False)


class Sum:
    def __init__(self, total, kind, order, relative, halved=None):
        self.total, self.kind, self.halved = total, kind, halved
        self.tail = total.shape[-2] - 16
        self.axes = list(range(total.ndim - 2))
        self.order, self.relative = order, relative

    def pack(self, step, shifts):
        axis = self.order[step]
        at = self.axes.index(axis)
        size = self.total.shape[at]
        me = 0
        if axis >= self.relative:
            me = (lax.axis_index("dp") >> shifts[axis]) & (size - 1)
        self.axes.pop(at)
        if self.halved is not None:
            self.keep, gives = self.halved[0], [self.halved[1]]
            self.halved = None
        else:
            self.keep = pick(self.total, at, me)
            gives = [pick(self.total, at, me ^ o) for o in range(1, size)]
        return [encode16(give, self.kind, self.tail) for give in gives]

    def swap(self, step, shifts, packs):
        shift = shifts[self.order[step]]
        return [dp_swap(p, (n + 1) << shift) for n, p in enumerate(packs)]

    def receive(self, gots):
        others = [decode16(g, self.kind, self.tail) for g in gots]
        total, top = self.keep, self.keep
        for other in others:
            total = total + other
            top = jnp.maximum(top, other)
        self.total = jnp.where(self.kind == 2.0, top + float(len(others)), total)


def split_lanes(packed, bounds, count):
    if count == 1:
        return packed
    blocks, rows, lanes = packed.shape
    plain = packed.reshape(blocks, rows, count, lanes // count)
    paired = packed.reshape(blocks, rows, 2, count, lanes // 2 // count)
    plain = jnp.moveaxis(plain, 2, 1)
    paired = jnp.moveaxis(paired, 3, 1).reshape(plain.shape)
    row = lax.broadcasted_iota(jnp.int32, plain.shape, 2)
    both = jnp.where((row >= bounds[0]) & (row < bounds[1]), paired, plain)
    return both.reshape(blocks * count, rows, lanes // count)


def per_device(fingerprints, w_first, w_second):
    tok, width = fingerprints.shape
    hid, emb = w_second.shape
    blk_count = lax.axis_size("blk")
    dp_count = lax.axis_size("dp")
    group_rows = tok * blk_count
    all_rows = group_rows * dp_count
    factor = 2.0 / math.sqrt(group_rows * all_rows)
    bits = dp_count.bit_length() - 1
    k = CHUNKS
    part = tok // k

    rem = []
    rows, own = lax.optimization_barrier((fingerprints[:part], fingerprints))
    rem.append(blk_swap(rows, 2))
    for start, count in ((1, k - 1),):
        names = [("rows", j) for j in range(start, start + count)]
        out = run(
            functools.partial(fetch, [("arg", j * part, part, ("rows", j)) for _, j in names]),
            {"arg": fingerprints},
            {name: ((part, width), BF16) for name in names},
            {"sems": pltpu.SemaphoreType.DMA((count,))},
            limit=2 << 20,
        )
        rem += [blk_swap(out[name], 2) for name in names]
    sib = blk_swap(own, 1)
    rs = []

    base = {"w_first": w_first, "w_second": w_second}
    out = run(
        first_stage,
        {**base, "own": fingerprints, "sib": sib},
        {
            "feats": ((2 * tok, width), BF16),
            "hidden": ((tok, hid), BF16),
            "gate": ((2, 256, tok), F32),
            "embed": ((2 * tok, emb), BF16),
            "sq": ((2 * tok, 128), F32),
            ("summed", 0): ((tok, emb), F32),
            "token": ((8, 128), F32),
        },
        {"pre": ((tok // 3, hid), F32), "hidden": ((tok // 3, hid), BF16)},
    )
    token = out["token"]
    hidden, gate, feats = [out["hidden"]], [out["gate"]], [out["feats"]]
    embed, sq, summed = [out["embed"]], [out["sq"]], [out["summed", 0]]
    feats, embed, sq, summed = {0: feats[0]}, {0: embed[0]}, {0: sq[0]}, summed
    half = part // 2
    for step in range(1, k + 1):
        out = run(
            split,
            {"rem": rem[step - 1], "token": token},
            {("rows", h): ((half, width), BF16) for h in range(2)},
            {},
            limit=2 << 20,
        )
        rs = [blk_swap(out["rows", h], 1) for h in range(2)]
        ins = {**base, "new": rem[step - 1]}
        for name in feats:
            if name == 0 or name[0] == "rs":
                ins["feats", name] = feats[name]
                ins["embed", name] = embed[name]
                ins["sq", name] = sq[name]
        embed_shape, sq_shape = ((part, emb), BF16), ((part, 128), F32)
        out = run(
            functools.partial(rem_stage, step),
            ins,
            {
                "hidden": ((part, hid), BF16),
                "gate": ((2, 256, part), F32),
                "embed": embed_shape,
                "total": ((part, emb), F32),
            },
            {"pre": ((part, hid), F32)},
        )
        hidden.append(out["hidden"])
        gate.append(out["gate"])
        name = ("rem", step)
        feats[name], embed[name] = rem[step - 1], out["embed"]

        ins = {**base, ("new", 0): rs[0], ("new", 1): rs[1], "total": out["total"]}
        for j in range(step + 1):
            name = ("rem", j) if j else 0
            ins["feats", name] = feats[name]
            ins["embed", name] = embed[name]
            if j < step:
                ins["sq", name] = sq[name]
                ins["summed", j] = summed[j]
        outs = {"feats": ((part, width), BF16)}
        scratch = {"both": ((2 * part, width), BF16), "embeds": ((2 * part, emb), BF16)}
        if step < k:
            outs = {**outs, "embed": embed_shape, "sq_rem": sq_shape, "sq_rs": sq_shape}
            outs["token"] = ((8, 128), F32)
            for j in range(step + 1):
                outs["summed", j] = ((tok if j == 0 else part, emb), F32)
            out = run(functools.partial(rs_stage, step), ins, outs, scratch)
            token = out["token"]
            summed = [out["summed", j] for j in range(step + 1)]
            name = ("rs", step)
            feats[name], embed[name], sq[name] = out["feats"], out["embed"], out["sq_rs"]
            sq["rem", step] = out["sq_rem"]
    rows = {}
    for j in range(k + 1):
        rows["hidden", j] = hidden[j]
        rows["gate", j] = gate[j]
    out = run(
        functools.partial(last_stage, factor),
        {**ins, **rows},
        {
            "feats": ((part, width), BF16),
            "dembed": ((2 * tok, emb), BF16),
            "quarters": ((4, 2 * tok, emb // 4), BF16),
            "give": ((256, 2 * tok), BF16),
            "second_give": ((emb // 4, hid), F32),
        },
        scratch,
    )
    feats["rs", k] = out["feats"]
    got = blk_swap(out["give"], 1)
    second_got = blk_swap(out["second_give"], 1)
    mine = {("feats", n): v for n, v in feats.items() if n == 0 or n[0] == "rem"}
    theirs = {("feats", n): v for n, v in feats.items() if n == 0 or n[0] == "rs"}
    own = run(
        own_share,
        {
            "w_second": w_second,
            "dembed": out["dembed"],
            "quarters": out["quarters"],
            **rows,
            **mine,
        },
        {
            "keep": ((256, 2 * tok), BF16),
            "second": ((emb // 4, hid), F32),
            "first": ((8, 256, 256), F32),
        },
        {},
    )
    rows_one, rows_two = CUT + 64 + 16, 256 - CUT + 16
    lanes = 256 * 8 // dp_count
    extra = dp_count // 8
    out = run(
        first_gradients,
        {
            "keep": own["keep"],
            "got": got,
            "second_keep": own["second"],
            "second_got": second_got,
            "first": own["first"],
            **theirs,
        },
        {
            "second": ((emb // 4, hid), F32),
            "exps": ((2, 8, 256), F32),
            "one": ((4, rows_one, 256), F32),
            "kind_one": ((rows_one, 256), F32),
            "kind_two": ((rows_two, 256), F32),
            "kind_all": ((336, 256), F32),
        },
        {},
    )
    kinds, one_give = (out["kind_one"], out["kind_two"], out["kind_all"]), out["one"]
    more = extra.bit_length() - 1
    shape = (2,) * more
    kind_one, kind_two = kinds[0][:, :lanes], kinds[1][:, :lanes]
    shifts = [more + 1, more] + [more - 1 - n for n in range(more)]
    rest = list(range(2, more + 2))
    cut = functools.partial(split_lanes, bounds=(CUT, CUT + 64), count=extra)
    one_give = cut(one_give).reshape((4,) + shape + (rows_one, lanes))
    early = encode16(one_give, kind_one, rows_one - 16)
    got, early = lax.optimization_barrier((got, early))
    out = run(
        other_gradients,
        {"got": got, "first": own["first"], "second": out["second"], "exps": out["exps"], **theirs},
        {"one": ((4, rows_one, 256), F32), "two": ((8, rows_two, 256), F32)},
        {},
    )
    one_keep = cut(out["one"]).reshape(one_give.shape)
    two = split_lanes(out["two"], (0, 0), extra).reshape((4, 2) + shape + (rows_two, lanes))
    one = Sum(jnp.stack([one_keep, one_give], 1), kind_one, [1, 0] + rest, 2, (one_keep, one_give))
    two = Sum(two, kind_two, [0] + rest + [1], 2)
    one.pack(0, shifts)
    gots_one = one.swap(0, shifts, [early])
    gots_two = two.swap(0, shifts, two.pack(0, shifts))
    for step in range(1, more + 2):
        one.receive(gots_one)
        packs = one.pack(step, shifts)
        gots_two, packs = lax.optimization_barrier((gots_two, packs))
        gots_one = one.swap(step, shifts, packs)
        gots_two, gots_one[0] = lax.optimization_barrier((gots_two, gots_one[0]))
        two.receive(gots_two)
        gots_two = two.swap(step, shifts, two.pack(step, shifts))
    one.receive(gots_one)
    two.receive(gots_two)
    if extra == 1:
        out = run(
            turn_quarter,
            {"one": one.total, "two": two.total},
            {"all": ((336, 256), F32)},
            {},
        )
        every = gather(encode16(out["all"], kinds[2], 320))
        out = run(
            place_quarters,
            {"all": decode16(every, kinds[2], 320)},
            {"first": ((lanes, hid), F32), "second": ((lanes // 2, emb), F32)},
            {},
        )
        return out["first"], out["second"]
    packed = [encode16(one.total, kind_one, one.tail), encode16(two.total, kind_two, two.tail)]
    every = gather(jnp.concatenate(packed, 0))
    one = decode16(every[:, :rows_one], kind_one, one.tail)
    two = decode16(every[:, rows_one:], kind_two, two.tail)
    order = jnp.arange(4) ^ lax.axis_index("blk")
    first = jnp.concatenate([one[:, :CUT], two[:, : 256 - CUT]], 1)[order].reshape(hid, lanes)
    second = one[order, CUT : CUT + 64]
    second = jnp.concatenate([second[..., : lanes // 2], second[..., lanes // 2 :]], 1)
    return first.T, second.reshape(emb, lanes // 2).T


def gather(packed):
    across = blk_swap(packed, 2)
    pair = jnp.stack([packed, across])
    beside = blk_swap(pair, 1)
    return jnp.stack([packed, beside[0], across, beside[1]])


def solution(mesh):
    in_specs = (P(("blk", "dp"), None), P(), P())
    out_specs = (P("dp", None), P("dp", None))
    return jax.shard_map(
        per_device, mesh=mesh, in_specs=in_specs, out_specs=out_specs, check_vma=False
    )
```

```python
import functools
import math

import jax
import jax.numpy as jnp
from jax import lax
from jax.experimental import pallas as pl
from jax.experimental.pallas import tpu as pltpu
from jax.sharding import PartitionSpec as P

F32 = jnp.float32
BF16 = jnp.bfloat16
F16 = jnp.float16
NN = (((1,), (0,)), ((), ()))
NT = (((1,), (1,)), ((), ()))
TN = (((0,), (0,)), ((), ()))
CHUNKS = 3
CUT = 240
VMEM_LIMIT = 20 * 1024 * 1024


def dot(left, right, dims=NN):
    return lax.dot_general(left, right, dims, preferred_element_type=F32)


def blk_swap(value, bit):
    count = lax.axis_size("blk")
    return lax.ppermute(value, "blk", [(b, b ^ bit) for b in range(count)])


def dp_swap(value, bit):
    count = lax.axis_size("dp")
    return lax.ppermute(value, "dp", [(d, d ^ bit) for d in range(count)])


def quarter_of(place, j):
    return pl.multiple_of((place ^ j) * 256, 256)


def encode(feats, w_first, w_second, pre_out=None, hidden_out=None):
    pre = dot(feats, w_first[...])
    hidden = (pre * jax.nn.sigmoid(pre)).astype(BF16)
    if pre_out is not None:
        pre_out[...] = pre
        hidden_out[...] = hidden
    return dot(hidden, w_second[...]).astype(BF16)


def put_gates(place, pre, out):
    for n in range(2):
        quarter = pre[:, pl.ds(quarter_of(place, n), 256)]
        sig = jax.nn.sigmoid(quarter)
        out[n] = (sig * (1.0 + quarter * (1.0 - sig))).T


def residual(inter, pred, sq_rows, sq_cols, emb):
    tanimoto = inter / (sq_rows + sq_cols - inter)
    return (pred * (1.0 / math.sqrt(emb)) - tanimoto).astype(BF16)


def first_stage(i, o, s):
    tok, emb = i["own"].shape[0], i["w_second"].shape[1]
    feats = o["feats"]
    feats[:tok] = i["own"][...]
    feats[tok:] = i["sib"][...]
    step = tok // 3
    for r in range(0, tok, step):
        rows = slice(r, r + step)
        embed = encode(feats[rows, :], i["w_first"], i["w_second"], s["pre"], s["hidden"])
        o["embed"][rows, :] = embed
        o["hidden"][rows, :] = s["hidden"][...]
        for n in range(2):
            quarter = s["pre"][:, pl.ds(quarter_of(lax.axis_index("blk"), n), 256)]
            sig = jax.nn.sigmoid(quarter)
            o["gate"][n, :, rows] = (sig * (1.0 + quarter * (1.0 - sig))).T
    for r in range(tok, 2 * tok, step):
        rows = slice(r, r + step)
        o["embed"][rows, :] = encode(feats[rows, :], i["w_first"], i["w_second"])
    embed = o["embed"][...]
    wide = feats[...].astype(F32)
    sq = jnp.broadcast_to(jnp.sum(wide * wide, axis=1, keepdims=True), o["sq"].shape)
    o["sq"][...] = sq
    sq_cols = sq.T[:1]
    inter = dot(feats[:tok], feats[...], NT)
    pred = dot(embed[:tok], embed, NT)
    resid = residual(inter, pred, sq[:tok, :1], sq_cols, emb)
    o["summed", 0][...] = dot(resid, embed)
    put_kinds(o)
    o["token"][...] = jnp.zeros((8, 128), F32)


def diagonals(square):
    at = lax.broadcasted_iota(jnp.int32, square.shape, 0)
    to = lax.broadcasted_iota(jnp.int32, square.shape, 1)
    only = jnp.where(at == to, square, 0.0)
    return jnp.sum(only, axis=1, keepdims=True), jnp.sum(only, axis=0, keepdims=True)


def rem_stage(k, i, o, s):
    emb = i["w_second"].shape[1]
    top = i["new"][...]
    embed_new = encode(top, i["w_first"], i["w_second"], s["pre"], o["hidden"])
    put_gates(lax.axis_index("blk"), s["pre"], o["gate"])
    o["embed"][...] = embed_new
    _, sq_cols = diagonals(dot(top, top, NT))
    tok = i["feats", 0].shape[0] // 2
    total = None
    for name in [0] + [("rs", j) for j in range(1, k)]:
        rows = pl.ds(tok, tok) if name == 0 else pl.ds(0, top.shape[0])
        old = i["embed", name][rows, :]
        inter = dot(i["feats", name][rows, :], top, NT)
        resid = residual(inter, dot(old, embed_new, NT), i["sq", name][rows, :1], sq_cols, emb)
        part = dot(resid, old, TN)
        total = part if total is None else total + part
    o["total"][...] = total


def rs_stage(k, i, o, s):
    emb = i["w_second"].shape[1]
    part = i["feats", ("rem", k)].shape[0]
    count = i["new", 0].shape[0]
    s["both"][:part] = i["feats", ("rem", k)][...]
    for h in range(part // count):
        s["both"][part + h * count : part + (h + 1) * count] = i["new", h][...]
    if "feats" in o:
        o["feats"][...] = s["both"][part:]
    embed_rs = encode(s["both"][part:], i["w_first"], i["w_second"])
    s["embeds"][:part] = i["embed", ("rem", k)][...]
    s["embeds"][part:] = embed_rs
    top, embed_new = s["both"][...], s["embeds"][...]
    inter = dot(top, top, NT)
    sq_rows, sq_cols = diagonals(inter)
    if "embed" in o:
        o["embed"][...] = embed_rs
        o["sq_rem"][...] = jnp.broadcast_to(sq_rows[:part], o["sq_rem"].shape)
        o["sq_rs"][...] = jnp.broadcast_to(sq_rows[part:], o["sq_rs"].shape)
        o["token"][...] = jnp.zeros((8, 128), F32)
    pred = dot(embed_new[:part], embed_new, NT)
    resid = residual(inter[:part], pred, sq_rows[:part], sq_cols, emb)
    total = i["total"][...] + dot(resid, embed_new)
    out = []
    for j in range(k):
        name = ("rem", j) if j else 0
        rows = pl.ds(0, i["summed", j].shape[0])
        old = i["embed", name][rows, :]
        inter = dot(i["feats", name][rows, :], top, NT)
        pred = dot(old, embed_new, NT)
        resid = residual(inter, pred, i["sq", name][rows, :1], sq_cols, emb)
        total += dot(resid[:, :part], old, TN)
        out.append(i["summed", j][...] + dot(resid, embed_new))
    out.append(total)
    for j in range(k + 1):
        if ("summed", j) in o:
            o["summed", j][...] = out[j]
    return out


def last_stage(factor, i, o, s):
    start = 0
    for value in rs_stage(CHUNKS, i, o, s):
        rows = pl.ds(start, value.shape[0])
        o["dembed"][rows, :] = (value * factor).astype(BF16)
        start += value.shape[0]
    dpre_share(lax.axis_index("blk"), 1, i, o["dembed"], o["give"])


def hiddens_of(i):
    return [i["hidden", j] for j in range(CHUNKS + 1)]


def dpre_share(place, n, i, dembed, out):
    turned = dot(i["w_second"][pl.ds(quarter_of(place, n), 256), :], dembed[...], NT)
    start = 0
    for j in range(CHUNKS + 1):
        gate = i["gate", j][n]
        rows = slice(start, start + gate.shape[1])
        out[:, rows] = (turned[:, rows] * gate).astype(BF16)
        start = rows.stop


def own_share(i, o, s):
    place = lax.axis_index("blk")
    dpre_share(place, 0, i, i["dembed"], o["keep"])
    for z in range(4):
        block = dp_high() ^ (2 * z + 1)
        o["first"][z] = first_block(o["keep"], core_rows(i, 0), block, 0, CUT)
    o["second_give"][...] = second_share(place ^ 1, i["dembed"], hiddens_of(i))


def put_kinds(o):
    for name, first, second in (("one", CUT, 0), ("two", 256 - CUT, 64), ("all", 256, 64)):
        kind = o["kind_" + name]
        kind[:first] = jnp.zeros((first, 256), F32)
        if second:
            kind[first : first + second] = jnp.ones((second, 256), F32)
        kind[first + second :] = jnp.full((16, 256), 2.0, F32)


def dp_high():
    return lax.axis_index("dp") // (lax.axis_size("dp") // 8)


def core_rows(i, core):
    both = i["feats", 0]
    tok = both.shape[0] // 2
    name = ("rem", "rs")[core]
    return [(both, core * tok, tok)] + [
        (i["feats", (name, j)], 0, i["feats", (name, j)].shape[0]) for j in range(1, CHUNKS + 1)
    ]


def first_block(dpre, rows, block, top=0, bottom=256):
    lanes = pl.ds(pl.multiple_of(block * 256, 256), 256)
    total, at = None, 0
    for ref, start, count in rows:
        piece = dot(dpre[top:bottom, at : at + count], ref[pl.ds(start, count), lanes])
        total = piece if total is None else total + piece
        at += count
    return total


def second_share(quarter, dembed, hiddens):
    total, start = None, 0
    columns = pl.ds(pl.multiple_of(quarter * 128, 128), 128)
    for hidden in hiddens:
        count = hidden.shape[0]
        part = dot(dembed[pl.ds(start, count), columns], hidden[...], TN)
        total = part if total is None else total + part
        start += count
    return total


def exponent(bound):
    return jnp.clip(jnp.ceil(jnp.log2(jnp.maximum(bound, 1e-30))) + 1.0, -100.0, 120.0)


def put_tail(ref, d, start, exp_first, exp_second):
    ref[d, start : start + 8] = exp_first
    ref[d, start + 8 : start + 16] = exp_second


def first_gradients(i, o, s):
    sums = jnp.sum(jnp.abs(i["keep"][...].astype(F32)), axis=1, keepdims=True)
    sums += jnp.sum(jnp.abs(i["got"][...].astype(F32)), axis=1, keepdims=True)
    top = exponent(3.0 * jnp.max(sums, axis=0, keepdims=True))
    o["exp_first"][...] = jnp.broadcast_to(top, (8, 256))
    for z in range(4):
        value = first_block(i["got"], core_rows(i, 1), dp_high() ^ (2 * z + 1), 0, CUT)
        o["one"][z, :CUT] = value + i["first"][z]
        put_tail(o["one"], z, CUT, o["exp_first"][...], o["exp_first"][...])


def second_gradients(i, o, s):
    me = dp_high()
    bottom = 256 - CUT
    mine = second_share(lax.axis_index("blk"), i["dembed"], hiddens_of(i))
    s["second"][...] = mine + i["second_got"][...]
    most = jnp.max(jnp.abs(s["second"][...]), axis=1, keepdims=True)
    exp_second = jnp.broadcast_to(exponent(jnp.max(most, axis=0, keepdims=True)), (8, 256))
    for d in range(8):
        value = first_block(i["keep"], core_rows(i, 0), me ^ d, CUT, 256)
        o["two"][d, :bottom] = value + first_block(i["got"], core_rows(i, 1), me ^ d, CUT, 256)
        second = s["second"][:, pl.ds(pl.multiple_of((me ^ d) * 128, 128), 128)]
        o["two"][d, bottom : bottom + 64, :128] = second[:64]
        o["two"][d, bottom : bottom + 64, 128:] = second[64:]
        put_tail(o["two"], d, bottom + 64, i["exp_first"][...], exp_second)


def kept_gradients(i, o, s):
    for z in range(4):
        block = dp_high() ^ (2 * z)
        value = first_block(i["keep"], core_rows(i, 0), block, 0, CUT)
        o["one"][z, :CUT] = value + first_block(i["got"], core_rows(i, 1), block, 0, CUT)
        put_tail(o["one"], z, CUT, i["exp_first"][...], i["exp_first"][...])


def run(body, ins, outs, scratch, limit=VMEM_LIMIT, to_hbm=False):
    names_in, names_out, names_s = list(ins), list(outs), list(scratch)

    def kernel(*refs):
        n, m = len(names_in), len(names_out)
        i = dict(zip(names_in, refs[:n]))
        o = dict(zip(names_out, refs[n : n + m]))
        body(i, o, dict(zip(names_s, refs[n + m :])))

    vmem = pltpu.VMEM
    spaces = {"arg": pl.ANY}
    shapes = [jax.ShapeDtypeStruct(*v) for v in outs.values()]
    got = pl.pallas_call(
        kernel,
        out_shape=shapes,
        in_specs=[pl.BlockSpec(memory_space=spaces.get(n, vmem)) for n in names_in],
        out_specs=[pl.BlockSpec(memory_space=pl.ANY if to_hbm else vmem)] * len(shapes),
        scratch_shapes=[vmem(*v) if isinstance(v, tuple) else v for v in scratch.values()],
        compiler_params=pltpu.CompilerParams(vmem_limit_bytes=limit),
        cost_estimate=pl.CostEstimate(flops=1, bytes_accessed=1, transcendentals=0),
    )(*ins.values())
    return dict(zip(names_out, got))


def split(i, o, s):
    count = i["rem"].shape[0] // len(o)
    for h in range(len(o)):
        o["rows", h][...] = i["rem"][h * count : (h + 1) * count]


def fetch(pairs, i, o, s):
    copies = []
    for n, (source, start, count, target) in enumerate(pairs):
        rows = i[source].at[pl.ds(start, count), :]
        copies.append(pltpu.make_async_copy(rows, o[target], s["sems"].at[n]))
        copies[-1].start()
    for copy in copies:
        copy.wait()


def turn_quarter(i, o, s):
    one, two, out = i["one"], i["two"], o["all"]
    bottom = 256 - CUT
    out[:256] = jnp.concatenate([one[:CUT], two[:bottom]], 0).T
    block = two[bottom : bottom + 64]
    second = jnp.concatenate([block[:, :128], block[:, 128:]], 0).T
    out[256:320, :128] = second[:64]
    out[256:320, 128:] = second[64:]
    lane = lax.broadcasted_iota(jnp.int32, (8, 256), 1)
    tail = two[bottom + 64 : bottom + 72]
    out[320:328] = jnp.where(lane < CUT, one[CUT : CUT + 8], tail)
    out[328:] = two[bottom + 72 :]


def place_quarters(i, o, s):
    me = lax.axis_index("blk")
    copies = []
    for j in range(4):
        q = me ^ j
        first = o["first"].at[:, pl.ds(pl.multiple_of(q * 256, 256), 256)]
        columns = pl.ds(pl.multiple_of(q * 128, 128), 128)
        pairs = [(i["all", j].at[pl.ds(0, 256), :], first)]
        for h in range(2):
            block = i["all", j].at[pl.ds(256, 64), pl.ds(128 * h, 128)]
            pairs.append((block, o["second"].at[pl.ds(64 * h, 64), columns]))
        for n, (source, target) in enumerate(pairs):
            copies.append(pltpu.make_async_copy(source, target, s["sems"].at[3 * j + n]))
            copies[-1].start()
    for copy in copies:
        copy.wait()


def encode16(total, kind, tail):
    first, second = [jnp.exp2(15.0 - e) for e in exps_of(total, tail)]
    scale = jnp.where(kind == 0.0, first, jnp.where(kind == 1.0, second, 1.0))
    return (total * scale).astype(F16)


def decode16(got, kind, tail):
    got = got.astype(F32)
    first, second = [jnp.exp2(e - 15.0) for e in exps_of(got, tail)]
    return got * jnp.where(kind == 0.0, first, jnp.where(kind == 1.0, second, 1.0))


def exps_of(value, tail):
    rows = value.ndim - 2
    return [lax.slice_in_dim(value, tail + at, tail + at + 1, axis=rows) for at in (0, 8)]


def halves(value, axis, mine):
    low = lax.index_in_dim(value, 0, axis, keepdims=False)
    high = lax.index_in_dim(value, 1, axis, keepdims=False)
    return jnp.where(mine == 0, low, high), jnp.where(mine == 0, high, low)


def pick(total, axis, index):
    if isinstance(index, int):
        return lax.index_in_dim(total, index, axis, keepdims=False)
    return lax.dynamic_index_in_dim(total, index, axis, keepdims=False)


class Sum:
    def __init__(self, total, kind, order, relative, halved=None):
        self.total, self.kind, self.halved = total, kind, halved
        self.tail = total.shape[-2] - 16
        self.axes = list(range(total.ndim - 2))
        self.order, self.relative = order, relative

    def pack(self, step, shifts):
        axis = self.order[step]
        at = self.axes.index(axis)
        size = self.total.shape[at]
        me = 0
        if axis >= self.relative:
            me = (lax.axis_index("dp") >> shifts[axis]) & (size - 1)
        self.axes.pop(at)
        if self.halved is not None:
            self.keep, gives = self.halved[0], [self.halved[1]]
            self.halved = None
        else:
            self.keep = pick(self.total, at, me)
            gives = [pick(self.total, at, me ^ o) for o in range(1, size)]
        return [encode16(give, self.kind, self.tail) for give in gives]

    def swap(self, step, shifts, packs):
        shift = shifts[self.order[step]]
        return [dp_swap(p, (n + 1) << shift) for n, p in enumerate(packs)]

    def receive(self, gots):
        others = [decode16(g, self.kind, self.tail) for g in gots]
        total, top = self.keep, self.keep
        for other in others:
            total = total + other
            top = jnp.maximum(top, other)
        self.total = jnp.where(self.kind == 2.0, top + float(len(others)), total)


def split_lanes(packed, bounds, count):
    if count == 1:
        return packed
    blocks, rows, lanes = packed.shape
    plain = packed.reshape(blocks, rows, count, lanes // count)
    paired = packed.reshape(blocks, rows, 2, count, lanes // 2 // count)
    plain = jnp.moveaxis(plain, 2, 1)
    paired = jnp.moveaxis(paired, 3, 1).reshape(plain.shape)
    row = lax.broadcasted_iota(jnp.int32, plain.shape, 2)
    both = jnp.where((row >= bounds[0]) & (row < bounds[1]), paired, plain)
    return both.reshape(blocks * count, rows, lanes // count)


def per_device(fingerprints, w_first, w_second):
    tok, width = fingerprints.shape
    hid, emb = w_second.shape
    blk_count = lax.axis_size("blk")
    dp_count = lax.axis_size("dp")
    group_rows = tok * blk_count
    all_rows = group_rows * dp_count
    factor = 2.0 / math.sqrt(group_rows * all_rows)
    bits = dp_count.bit_length() - 1
    k = CHUNKS
    part = tok // k
    rows_one, rows_two = CUT + 16, 256 - CUT + 64 + 16
    lanes = 256 * 8 // dp_count
    extra = dp_count // 8

    rows, own = lax.optimization_barrier((fingerprints[:part], fingerprints))
    rem = [blk_swap(rows, 2)]
    out = run(
        functools.partial(fetch, [("arg", j * part, part, ("rows", j)) for j in range(1, k)]),
        {"arg": fingerprints},
        {("rows", j): ((part, width), BF16) for j in range(1, k)},
        {"sems": pltpu.SemaphoreType.DMA((k - 1,))},
        limit=2 << 20,
    )
    rem += [blk_swap(out["rows", j], 2) for j in range(1, k)]
    sib = blk_swap(own, 1)
    base = {"w_first": w_first, "w_second": w_second}
    out = run(
        first_stage,
        {**base, "own": fingerprints, "sib": sib},
        {
            "feats": ((2 * tok, width), BF16),
            "hidden": ((tok, hid), BF16),
            "gate": ((2, 256, tok), F32),
            "embed": ((2 * tok, emb), BF16),
            "sq": ((2 * tok, 128), F32),
            ("summed", 0): ((tok, emb), F32),
            "token": ((8, 128), F32),
            "kind_one": ((rows_one, 256), F32),
            "kind_two": ((rows_two, 256), F32),
            "kind_all": ((336, 256), F32),
        },
        {"pre": ((tok // 3, hid), F32), "hidden": ((tok // 3, hid), BF16)},
    )
    token = out["token"]
    kinds = [out["kind_one"], out["kind_two"], out["kind_all"]]
    hidden, gate, feats = [out["hidden"]], [out["gate"]], [out["feats"]]
    embed, sq, summed = [out["embed"]], [out["sq"]], [out["summed", 0]]
    feats, embed, sq, summed = {0: feats[0]}, {0: embed[0]}, {0: sq[0]}, summed
    for step in range(1, k + 1):
        pieces = 2 if step < k else 1
        out = run(
            split,
            {"rem": rem[step - 1], "token": token},
            {("rows", h): ((part // pieces, width), BF16) for h in range(pieces)},
            {},
            limit=2 << 20,
        )
        rs = [blk_swap(out["rows", h], 1) for h in range(pieces)]
        ins = {**base, "new": rem[step - 1]}
        for name in feats:
            if name == 0 or name[0] == "rs":
                ins["feats", name] = feats[name]
                ins["embed", name] = embed[name]
                ins["sq", name] = sq[name]
        embed_shape, sq_shape = ((part, emb), BF16), ((part, 128), F32)
        out = run(
            functools.partial(rem_stage, step),
            ins,
            {
                "hidden": ((part, hid), BF16),
                "gate": ((2, 256, part), F32),
                "embed": embed_shape,
                "total": ((part, emb), F32),
            },
            {"pre": ((part, hid), F32)},
        )
        hidden.append(out["hidden"])
        gate.append(out["gate"])
        name = ("rem", step)
        feats[name], embed[name] = rem[step - 1], out["embed"]

        ins = {**base, **{("new", h): r for h, r in enumerate(rs)}, "total": out["total"]}
        for j in range(step + 1):
            name = ("rem", j) if j else 0
            ins["feats", name] = feats[name]
            ins["embed", name] = embed[name]
            if j < step:
                ins["sq", name] = sq[name]
                ins["summed", j] = summed[j]
        outs = {"feats": ((part, width), BF16)}
        scratch = {"both": ((2 * part, width), BF16), "embeds": ((2 * part, emb), BF16)}
        if step < k:
            outs = {**outs, "embed": embed_shape, "sq_rem": sq_shape, "sq_rs": sq_shape}
            outs["token"] = ((8, 128), F32)
            for j in range(step + 1):
                outs["summed", j] = ((tok if j == 0 else part, emb), F32)
            out = run(functools.partial(rs_stage, step), ins, outs, scratch)
            token = out["token"]
            summed = [out["summed", j] for j in range(step + 1)]
            name = ("rs", step)
            feats[name], embed[name], sq[name] = out["feats"], out["embed"], out["sq_rs"]
            sq["rem", step] = out["sq_rem"]
    rows = {}
    for j in range(k + 1):
        rows["hidden", j] = hidden[j]
        rows["gate", j] = gate[j]
    out = run(
        functools.partial(last_stage, factor),
        {**ins, **rows},
        {
            "dembed": ((2 * tok, emb), BF16),
            "give": ((256, 2 * tok), BF16),
        },
        scratch,
    )
    feats["rs", k] = rs[0]
    got = blk_swap(out["give"], 1)
    mine = {("feats", n): v for n, v in feats.items() if n == 0 or n[0] == "rem"}
    theirs = {("feats", n): v for n, v in feats.items() if n == 0 or n[0] == "rs"}
    dembed = out["dembed"]
    own = run(
        own_share,
        {"w_second": w_second, "dembed": dembed, **rows, **mine},
        {
            "keep": ((256, 2 * tok), BF16),
            "second_give": ((emb // 4, hid), F32),
            "first": ((4, CUT, 256), F32),
        },
        {},
    )
    second_got = blk_swap(own["second_give"], 1)
    out = run(
        first_gradients,
        {"keep": own["keep"], "got": got, "first": own["first"], **theirs},
        {"one": ((4, rows_one, 256), F32), "exp_first": ((8, 256), F32)},
        {},
    )
    one_give = out["one"]
    more = extra.bit_length() - 1
    shape = (2,) * more
    kind_one, kind_two = kinds[0][:, :lanes], kinds[1][:, :lanes]
    shifts = [more + 1, more] + [more - 1 - n for n in range(more)]
    rest = list(range(2, more + 2))
    cut = functools.partial(split_lanes, bounds=(0, 0), count=extra)
    one_give = cut(one_give).reshape((4,) + shape + (rows_one, lanes))
    early = encode16(one_give, kind_one, rows_one - 16)
    got, early = lax.optimization_barrier((got, early))
    ins = {"keep": own["keep"], "got": got, "exp_first": out["exp_first"], **mine, **theirs}
    out = run(
        second_gradients,
        {
            **ins,
            "dembed": dembed,
            "second_got": second_got,
            **{n: v for n, v in rows.items() if n[0] == "hidden"},
        },
        {"two": ((8, rows_two, 256), F32)},
        {"second": ((emb // 4, hid), F32)},
    )
    two = split_lanes(out["two"], (256 - CUT, 320 - CUT), extra)
    two = Sum(two.reshape((4, 2) + shape + (rows_two, lanes)), kind_two, [0] + rest + [1], 2)
    packs_two = two.pack(0, shifts)
    ins["got"], packs_two = lax.optimization_barrier((got, packs_two))
    kept = run(kept_gradients, ins, {"one": ((4, rows_one, 256), F32)}, {})
    one_keep = cut(kept["one"]).reshape(one_give.shape)
    one = Sum(jnp.stack([one_keep, one_give], 1), kind_one, [1, 0] + rest, 2, (one_keep, one_give))
    one.pack(0, shifts)
    gots_one = one.swap(0, shifts, [early])
    gots_two = two.swap(0, shifts, packs_two)
    for step in range(1, more + 2):
        one.receive(gots_one)
        packs = one.pack(step, shifts)
        gots_two, packs = lax.optimization_barrier((gots_two, packs))
        gots_one = one.swap(step, shifts, packs)
        gots_two, gots_one[0] = lax.optimization_barrier((gots_two, gots_one[0]))
        two.receive(gots_two)
        gots_two = two.swap(step, shifts, two.pack(step, shifts))
    one.receive(gots_one)
    two.receive(gots_two)
    if extra == 1:
        out = run(
            turn_quarter,
            {"one": one.total, "two": two.total},
            {"all": ((336, 256), F32)},
            {},
        )
        four = [out["all"]]
        four += [decode16(g, kinds[2], 320) for g in gather(encode16(out["all"], kinds[2], 320))[1:]]
        out = run(
            place_quarters,
            {("all", j): v for j, v in enumerate(four)},
            {"first": ((lanes, hid), F32), "second": ((lanes // 2, emb), F32)},
            {"sems": pltpu.SemaphoreType.DMA((12,))},
            to_hbm=True,
        )
        return out["first"], out["second"]
    packed = [encode16(one.total, kind_one, one.tail), encode16(two.total, kind_two, two.tail)]
    every = jnp.stack(gather(jnp.concatenate(packed, 0)))
    one = decode16(every[:, :rows_one], kind_one, one.tail)
    two = decode16(every[:, rows_one:], kind_two, two.tail)
    order = jnp.arange(4) ^ lax.axis_index("blk")
    first = jnp.concatenate([one[:, :CUT], two[:, : 256 - CUT]], 1)[order].reshape(hid, lanes)
    second = two[order, 256 - CUT : 320 - CUT]
    second = jnp.concatenate([second[..., : lanes // 2], second[..., lanes // 2 :]], 1)
    return first.T, second.reshape(emb, lanes // 2).T


def gather(packed):
    across = blk_swap(packed, 2)
    pair = jnp.stack([packed, across])
    beside = blk_swap(pair, 1)
    return [packed, beside[0], across, beside[1]]


def solution(mesh):
    in_specs = (P(("blk", "dp"), None), P(), P())
    out_specs = (P("dp", None), P("dp", None))
    return jax.shard_map(
        per_device, mesh=mesh, in_specs=in_specs, out_specs=out_specs, check_vma=False
    )
```

```python
import functools
import math

import jax
import jax.numpy as jnp
from jax import lax
from jax.experimental import pallas as pl
from jax.experimental.pallas import tpu as pltpu
from jax.sharding import PartitionSpec as P

F32 = jnp.float32
BF16 = jnp.bfloat16
F16 = jnp.float16
NN = (((1,), (0,)), ((), ()))
NT = (((1,), (1,)), ((), ()))
TN = (((0,), (0,)), ((), ()))
CHUNKS = 3
CUT = 240
VMEM_LIMIT = 20 * 1024 * 1024


def dot(left, right, dims=NN):
    return lax.dot_general(left, right, dims, preferred_element_type=F32)


def blk_swap(value, bit):
    count = lax.axis_size("blk")
    return lax.ppermute(value, "blk", [(b, b ^ bit) for b in range(count)])


def dp_swap(value, bit):
    count = lax.axis_size("dp")
    return lax.ppermute(value, "dp", [(d, d ^ bit) for d in range(count)])


def quarter_of(place, j):
    return pl.multiple_of((place ^ j) * 256, 256)


def encode(feats, w_first, w_second, pre_out=None, hidden_out=None):
    pre = dot(feats, w_first[...])
    hidden = (pre * jax.nn.sigmoid(pre)).astype(BF16)
    if pre_out is not None:
        pre_out[...] = pre
        hidden_out[...] = hidden
    return dot(hidden, w_second[...]).astype(BF16)


def put_gates(place, pre, out):
    for n in range(2):
        quarter = pre[:, pl.ds(quarter_of(place, n), 256)]
        sig = jax.nn.sigmoid(quarter)
        out[n] = (sig * (1.0 + quarter * (1.0 - sig))).T


def residual(inter, pred, sq_rows, sq_cols, emb):
    tanimoto = inter / (sq_rows + sq_cols - inter)
    return (pred * (1.0 / math.sqrt(emb)) - tanimoto).astype(BF16)


def first_stage(i, o, s):
    tok, emb = i["own"].shape[0], i["w_second"].shape[1]
    feats = o["feats"]
    feats[:tok] = i["own"][...]
    feats[tok:] = i["sib"][...]
    step = tok // 3
    for r in range(0, tok, step):
        rows = slice(r, r + step)
        embed = encode(feats[rows, :], i["w_first"], i["w_second"], s["pre"], s["hidden"])
        o["embed"][rows, :] = embed
        o["hidden"][rows, :] = s["hidden"][...]
        for n in range(2):
            quarter = s["pre"][:, pl.ds(quarter_of(lax.axis_index("blk"), n), 256)]
            sig = jax.nn.sigmoid(quarter)
            o["gate"][n, :, rows] = (sig * (1.0 + quarter * (1.0 - sig))).T
    for r in range(tok, 2 * tok, step):
        rows = slice(r, r + step)
        o["embed"][rows, :] = encode(feats[rows, :], i["w_first"], i["w_second"])
    embed = o["embed"][...]
    wide = feats[...].astype(F32)
    sq = jnp.broadcast_to(jnp.sum(wide * wide, axis=1, keepdims=True), o["sq"].shape)
    o["sq"][...] = sq
    sq_cols = sq.T[:1]
    inter = dot(feats[:tok], feats[...], NT)
    pred = dot(embed[:tok], embed, NT)
    resid = residual(inter, pred, sq[:tok, :1], sq_cols, emb)
    o["summed", 0][...] = dot(resid, embed)
    put_kinds(o)
    o["token"][...] = jnp.zeros((8, 128), F32)


def diagonals(square):
    at = lax.broadcasted_iota(jnp.int32, square.shape, 0)
    to = lax.broadcasted_iota(jnp.int32, square.shape, 1)
    only = jnp.where(at == to, square, 0.0)
    return jnp.sum(only, axis=1, keepdims=True), jnp.sum(only, axis=0, keepdims=True)


def rem_stage(k, i, o, s):
    emb = i["w_second"].shape[1]
    top = i["new"][...]
    embed_new = encode(top, i["w_first"], i["w_second"], s["pre"], o["hidden"])
    put_gates(lax.axis_index("blk"), s["pre"], o["gate"])
    o["embed"][...] = embed_new
    _, sq_cols = diagonals(dot(top, top, NT))
    tok = i["feats", 0].shape[0] // 2
    total = None
    for name in names_of(k, "rs"):
        rows = pl.ds(tok, tok) if name == 0 else pl.ds(0, i["sq", name].shape[0])
        old = i["embed", name][rows, :]
        inter = dot(i["feats", name][rows, :], top, NT)
        resid = residual(inter, dot(old, embed_new, NT), i["sq", name][rows, :1], sq_cols, emb)
        part = dot(resid, old, TN)
        total = part if total is None else total + part
    o["total"][...] = total


def rs_stage(k, i, o, s):
    emb = i["w_second"].shape[1]
    part = i["feats", ("rem", k)].shape[0]
    count = i["new", 0].shape[0]
    s["both"][:part] = i["feats", ("rem", k)][...]
    for h in range(part // count):
        s["both"][part + h * count : part + (h + 1) * count] = i["new", h][...]
    if "feats" in o:
        o["feats"][...] = s["both"][part:]
    embed_rs = encode(s["both"][part:], i["w_first"], i["w_second"])
    s["embeds"][:part] = i["embed", ("rem", k)][...]
    s["embeds"][part:] = embed_rs
    top, embed_new = s["both"][...], s["embeds"][...]
    inter = dot(top, top, NT)
    sq_rows, sq_cols = diagonals(inter)
    if "embed" in o:
        o["embed"][...] = embed_rs
        o["sq_rem"][...] = jnp.broadcast_to(sq_rows[:part], o["sq_rem"].shape)
        o["sq_rs"][...] = jnp.broadcast_to(sq_rows[part:], o["sq_rs"].shape)
        o["token"][...] = jnp.zeros((8, 128), F32)
    pred = dot(embed_new[:part], embed_new, NT)
    resid = residual(inter[:part], pred, sq_rows[:part], sq_cols, emb)
    total = i["total"][...] + dot(resid, embed_new)
    out = []
    for name in names_of(k, "rem"):
        rows = pl.ds(0, i["summed", name].shape[0])
        old = i["embed", name][rows, :]
        inter = dot(i["feats", name][rows, :], top, NT)
        pred = dot(old, embed_new, NT)
        resid = residual(inter, pred, i["sq", name][rows, :1], sq_cols, emb)
        total += dot(resid[:, :part], old, TN)
        out.append(i["summed", name][...] + dot(resid, embed_new))
    out.append(total)
    for name, value in zip(names_of(k, "rem") + [("rem", k)], out):
        if ("summed", name) in o:
            o["summed", name][...] = value
    return out


def names_of(k, kind):
    if k == CHUNKS:
        return [0, (kind, 0)]
    return [0] + [(kind, j) for j in range(1, k)]


def join(i, o, s):
    for target, out in o.items():
        if target == "token":
            out[...] = jnp.zeros((8, 128), F32)
            continue
        what, (kind, _) = target
        start = 0
        for j in range(1, CHUNKS):
            count = i[what, (kind, j)].shape[0]
            out[start : start + count] = i[what, (kind, j)][...]
            start += count


def last_stage(factor, i, o, s):
    start = 0
    for value in rs_stage(CHUNKS, i, o, s):
        rows = pl.ds(start, value.shape[0])
        o["dembed"][rows, :] = (value * factor).astype(BF16)
        start += value.shape[0]
    dpre_share(lax.axis_index("blk"), 1, i, o["dembed"], o["give"])


def hiddens_of(i):
    return [i["hidden", j] for j in range(CHUNKS + 1)]


def dpre_share(place, n, i, dembed, out):
    turned = dot(i["w_second"][pl.ds(quarter_of(place, n), 256), :], dembed[...], NT)
    start = 0
    for j in range(CHUNKS + 1):
        gate = i["gate", j][n]
        rows = slice(start, start + gate.shape[1])
        out[:, rows] = (turned[:, rows] * gate).astype(BF16)
        start = rows.stop


def own_share(i, o, s):
    place = lax.axis_index("blk")
    dpre_share(place, 0, i, i["dembed"], o["keep"])
    for z in range(4):
        block = dp_high() ^ (2 * z + 1)
        o["first"][z] = first_block(o["keep"], core_rows(i, 0), block, 0, CUT)
    o["second_give"][...] = second_share(place ^ 1, i["dembed"], hiddens_of(i))


def put_kinds(o):
    for name, first, second in (("one", CUT, 0), ("two", 256 - CUT, 64), ("all", 256, 64)):
        kind = o["kind_" + name]
        kind[:first] = jnp.zeros((first, 256), F32)
        if second:
            kind[first : first + second] = jnp.ones((second, 256), F32)
        kind[first + second :] = jnp.full((16, 256), 2.0, F32)


def dp_high():
    return lax.axis_index("dp") // (lax.axis_size("dp") // 8)


def core_rows(i, core):
    tok = i["feats", 0].shape[0] // 2
    kind = ("rem", "rs")[core]
    return [(i["feats", 0], core * tok, tok)] + [
        (i["feats", (kind, j)], 0, i["feats", (kind, j)].shape[0]) for j in (0, CHUNKS)
    ]


def first_block(dpre, rows, block, top=0, bottom=256):
    lanes = pl.ds(pl.multiple_of(block * 256, 256), 256)
    total, at = None, 0
    for ref, start, count in rows:
        piece = dot(dpre[top:bottom, at : at + count], ref[pl.ds(start, count), lanes])
        total = piece if total is None else total + piece
        at += count
    return total


def second_share(quarter, dembed, hiddens):
    total, start = None, 0
    columns = pl.ds(pl.multiple_of(quarter * 128, 128), 128)
    for hidden in hiddens:
        count = hidden.shape[0]
        part = dot(dembed[pl.ds(start, count), columns], hidden[...], TN)
        total = part if total is None else total + part
        start += count
    return total


def exponent(bound):
    return jnp.clip(jnp.ceil(jnp.log2(jnp.maximum(bound, 1e-30))) + 1.0, -100.0, 120.0)


def put_tail(ref, d, start, exp_first, exp_second):
    ref[d, start : start + 8] = exp_first
    ref[d, start + 8 : start + 16] = exp_second


def first_gradients(i, o, s):
    sums = jnp.sum(jnp.abs(i["keep"][...].astype(F32)), axis=1, keepdims=True)
    sums += jnp.sum(jnp.abs(i["got"][...].astype(F32)), axis=1, keepdims=True)
    top = exponent(3.0 * jnp.max(sums, axis=0, keepdims=True))
    o["exp_first"][...] = jnp.broadcast_to(top, (8, 256))
    for z in range(4):
        value = first_block(i["got"], core_rows(i, 1), dp_high() ^ (2 * z + 1), 0, CUT)
        o["one"][z, :CUT] = value + i["first"][z]
        put_tail(o["one"], z, CUT, o["exp_first"][...], o["exp_first"][...])


def second_gradients(i, o, s):
    me = dp_high()
    bottom = 256 - CUT
    mine = second_share(lax.axis_index("blk"), i["dembed"], hiddens_of(i))
    s["second"][...] = mine + i["second_got"][...]
    most = jnp.max(jnp.abs(s["second"][...]), axis=1, keepdims=True)
    exp_second = jnp.broadcast_to(exponent(jnp.max(most, axis=0, keepdims=True)), (8, 256))
    for d in range(8):
        value = first_block(i["keep"], core_rows(i, 0), me ^ d, CUT, 256)
        o["two"][d, :bottom] = value + first_block(i["got"], core_rows(i, 1), me ^ d, CUT, 256)
        second = s["second"][:, pl.ds(pl.multiple_of((me ^ d) * 128, 128), 128)]
        o["two"][d, bottom : bottom + 64, :128] = second[:64]
        o["two"][d, bottom : bottom + 64, 128:] = second[64:]
        put_tail(o["two"], d, bottom + 64, i["exp_first"][...], exp_second)


def kept_gradients(i, o, s):
    for z in range(4):
        block = dp_high() ^ (2 * z)
        value = first_block(i["keep"], core_rows(i, 0), block, 0, CUT)
        o["one"][z, :CUT] = value + first_block(i["got"], core_rows(i, 1), block, 0, CUT)
        put_tail(o["one"], z, CUT, i["exp_first"][...], i["exp_first"][...])


def run(body, ins, outs, scratch, limit=VMEM_LIMIT, to_hbm=False):
    names_in, names_out, names_s = list(ins), list(outs), list(scratch)

    def kernel(*refs):
        n, m = len(names_in), len(names_out)
        i = dict(zip(names_in, refs[:n]))
        o = dict(zip(names_out, refs[n : n + m]))
        body(i, o, dict(zip(names_s, refs[n + m :])))

    vmem = pltpu.VMEM
    spaces = {"arg": pl.ANY}
    shapes = [jax.ShapeDtypeStruct(*v) for v in outs.values()]
    got = pl.pallas_call(
        kernel,
        out_shape=shapes,
        in_specs=[pl.BlockSpec(memory_space=spaces.get(n, vmem)) for n in names_in],
        out_specs=[pl.BlockSpec(memory_space=pl.ANY if to_hbm else vmem)] * len(shapes),
        scratch_shapes=[vmem(*v) if isinstance(v, tuple) else v for v in scratch.values()],
        compiler_params=pltpu.CompilerParams(vmem_limit_bytes=limit),
        cost_estimate=pl.CostEstimate(flops=1, bytes_accessed=1, transcendentals=0),
    )(*ins.values())
    return dict(zip(names_out, got))


def split(i, o, s):
    count = i["rem"].shape[0] // len(o)
    for h in range(len(o)):
        o["rows", h][...] = i["rem"][h * count : (h + 1) * count]


def fetch(pairs, i, o, s):
    copies = []
    for n, (source, start, count, target) in enumerate(pairs):
        rows = i[source].at[pl.ds(start, count), :]
        copies.append(pltpu.make_async_copy(rows, o[target], s["sems"].at[n]))
        copies[-1].start()
    for copy in copies:
        copy.wait()


def turn_quarter(i, o, s):
    one, two, out = i["one"], i["two"], o["all"]
    bottom = 256 - CUT
    out[:256] = jnp.concatenate([one[:CUT], two[:bottom]], 0).T
    block = two[bottom : bottom + 64]
    second = jnp.concatenate([block[:, :128], block[:, 128:]], 0).T
    out[256:320, :128] = second[:64]
    out[256:320, 128:] = second[64:]
    lane = lax.broadcasted_iota(jnp.int32, (8, 256), 1)
    tail = two[bottom + 64 : bottom + 72]
    out[320:328] = jnp.where(lane < CUT, one[CUT : CUT + 8], tail)
    out[328:] = two[bottom + 72 :]


def place_quarters(i, o, s):
    me = lax.axis_index("blk")
    copies = []
    for j in range(4):
        q = me ^ j
        first = o["first"].at[:, pl.ds(pl.multiple_of(q * 256, 256), 256)]
        columns = pl.ds(pl.multiple_of(q * 128, 128), 128)
        pairs = [(i["all", j].at[pl.ds(0, 256), :], first)]
        for h in range(2):
            block = i["all", j].at[pl.ds(256, 64), pl.ds(128 * h, 128)]
            pairs.append((block, o["second"].at[pl.ds(64 * h, 64), columns]))
        for n, (source, target) in enumerate(pairs):
            copies.append(pltpu.make_async_copy(source, target, s["sems"].at[3 * j + n]))
            copies[-1].start()
    for copy in copies:
        copy.wait()


def encode16(total, kind, tail):
    first, second = [jnp.exp2(15.0 - e) for e in exps_of(total, tail)]
    scale = jnp.where(kind == 0.0, first, jnp.where(kind == 1.0, second, 1.0))
    return (total * scale).astype(F16)


def decode16(got, kind, tail):
    got = got.astype(F32)
    first, second = [jnp.exp2(e - 15.0) for e in exps_of(got, tail)]
    return got * jnp.where(kind == 0.0, first, jnp.where(kind == 1.0, second, 1.0))


def exps_of(value, tail):
    rows = value.ndim - 2
    return [lax.slice_in_dim(value, tail + at, tail + at + 1, axis=rows) for at in (0, 8)]


def halves(value, axis, mine):
    low = lax.index_in_dim(value, 0, axis, keepdims=False)
    high = lax.index_in_dim(value, 1, axis, keepdims=False)
    return jnp.where(mine == 0, low, high), jnp.where(mine == 0, high, low)


def pick(total, axis, index):
    if isinstance(index, int):
        return lax.index_in_dim(total, index, axis, keepdims=False)
    return lax.dynamic_index_in_dim(total, index, axis, keepdims=False)


class Sum:
    def __init__(self, total, kind, order, relative, halved=None):
        self.total, self.kind, self.halved = total, kind, halved
        self.tail = total.shape[-2] - 16
        self.axes = list(range(total.ndim - 2))
        self.order, self.relative = order, relative

    def pack(self, step, shifts):
        axis = self.order[step]
        at = self.axes.index(axis)
        size = self.total.shape[at]
        me = 0
        if axis >= self.relative:
            me = (lax.axis_index("dp") >> shifts[axis]) & (size - 1)
        self.axes.pop(at)
        if self.halved is not None:
            self.keep, gives = self.halved[0], [self.halved[1]]
            self.halved = None
        else:
            self.keep = pick(self.total, at, me)
            gives = [pick(self.total, at, me ^ o) for o in range(1, size)]
        return [encode16(give, self.kind, self.tail) for give in gives]

    def swap(self, step, shifts, packs):
        shift = shifts[self.order[step]]
        return [dp_swap(p, (n + 1) << shift) for n, p in enumerate(packs)]

    def receive(self, gots):
        others = [decode16(g, self.kind, self.tail) for g in gots]
        total, top = self.keep, self.keep
        for other in others:
            total = total + other
            top = jnp.maximum(top, other)
        self.total = jnp.where(self.kind == 2.0, top + float(len(others)), total)


def split_lanes(packed, bounds, count):
    if count == 1:
        return packed
    blocks, rows, lanes = packed.shape
    plain = packed.reshape(blocks, rows, count, lanes // count)
    paired = packed.reshape(blocks, rows, 2, count, lanes // 2 // count)
    plain = jnp.moveaxis(plain, 2, 1)
    paired = jnp.moveaxis(paired, 3, 1).reshape(plain.shape)
    row = lax.broadcasted_iota(jnp.int32, plain.shape, 2)
    both = jnp.where((row >= bounds[0]) & (row < bounds[1]), paired, plain)
    return both.reshape(blocks * count, rows, lanes // count)


def per_device(fingerprints, w_first, w_second):
    tok, width = fingerprints.shape
    hid, emb = w_second.shape
    blk_count = lax.axis_size("blk")
    dp_count = lax.axis_size("dp")
    group_rows = tok * blk_count
    all_rows = group_rows * dp_count
    factor = 2.0 / math.sqrt(group_rows * all_rows)
    bits = dp_count.bit_length() - 1
    k = CHUNKS
    part = tok // k
    rows_one, rows_two = CUT + 16, 256 - CUT + 64 + 16
    lanes = 256 * 8 // dp_count
    extra = dp_count // 8

    rows, own = lax.optimization_barrier((fingerprints[:part], fingerprints))
    rem = [blk_swap(rows, 2)]
    out = run(
        functools.partial(fetch, [("arg", j * part, part, ("rows", j)) for j in range(1, k)]),
        {"arg": fingerprints},
        {("rows", j): ((part, width), BF16) for j in range(1, k)},
        {"sems": pltpu.SemaphoreType.DMA((k - 1,))},
        limit=2 << 20,
    )
    rem += [blk_swap(out["rows", j], 2) for j in range(1, k)]
    sib = blk_swap(own, 1)
    base = {"w_first": w_first, "w_second": w_second}
    out = run(
        first_stage,
        {**base, "own": fingerprints, "sib": sib},
        {
            "feats": ((2 * tok, width), BF16),
            "hidden": ((tok, hid), BF16),
            "gate": ((2, 256, tok), F32),
            "embed": ((2 * tok, emb), BF16),
            "sq": ((2 * tok, 128), F32),
            ("summed", 0): ((tok, emb), F32),
            "token": ((8, 128), F32),
            "kind_one": ((rows_one, 256), F32),
            "kind_two": ((rows_two, 256), F32),
            "kind_all": ((336, 256), F32),
        },
        {"pre": ((tok // 3, hid), F32), "hidden": ((tok // 3, hid), BF16)},
    )
    token = out["token"]
    kinds = [out["kind_one"], out["kind_two"], out["kind_all"]]
    hidden, gate, feats = [out["hidden"]], [out["gate"]], [out["feats"]]
    embed, sq, summed = [out["embed"]], [out["sq"]], [out["summed", 0]]
    feats, embed, sq, summed = {0: feats[0]}, {0: embed[0]}, {0: sq[0]}, {0: summed[0]}
    for step in range(1, k + 1):
        if step == k:
            ins, outs = {}, {"token": ((8, 128), F32)}
            for kind in ("rem", "rs"):
                for what, values in (("feats", feats), ("embed", embed), ("sq", sq), ("summed", summed)):
                    if what == "summed" and kind == "rs":
                        continue
                    for j in range(1, k):
                        ins[what, (kind, j)] = values[kind, j]
                    count, lanes_of = values[kind, 1].shape
                    outs[what, (kind, 0)] = ((count * (k - 1), lanes_of), values[kind, 1].dtype)
            ins["token"] = token
            joined = run(join, ins, outs, {})
            token = joined["token"]
            for target, value in joined.items():
                if target != "token":
                    {"feats": feats, "embed": embed, "sq": sq, "summed": summed}[target[0]][
                        target[1]
                    ] = value
        pieces = 2 if step < k else 1
        out = run(
            split,
            {"rem": rem[step - 1], "token": token},
            {("rows", h): ((part // pieces, width), BF16) for h in range(pieces)},
            {},
            limit=2 << 20,
        )
        rs = [blk_swap(out["rows", h], 1) for h in range(pieces)]
        ins = {**base, "new": rem[step - 1]}
        for name in names_of(step, "rs"):
            ins["feats", name] = feats[name]
            ins["embed", name] = embed[name]
            ins["sq", name] = sq[name]
        embed_shape, sq_shape = ((part, emb), BF16), ((part, 128), F32)
        out = run(
            functools.partial(rem_stage, step),
            ins,
            {
                "hidden": ((part, hid), BF16),
                "gate": ((2, 256, part), F32),
                "embed": embed_shape,
                "total": ((part, emb), F32),
            },
            {"pre": ((part, hid), F32)},
        )
        hidden.append(out["hidden"])
        gate.append(out["gate"])
        name = ("rem", step)
        feats[name], embed[name] = rem[step - 1], out["embed"]

        ins = {**base, **{("new", h): r for h, r in enumerate(rs)}, "total": out["total"]}
        for name in names_of(step, "rem") + [("rem", step)]:
            ins["feats", name] = feats[name]
            ins["embed", name] = embed[name]
            if name != ("rem", step):
                ins["sq", name] = sq[name]
                ins["summed", name] = summed[name]
        outs = {"feats": ((part, width), BF16)}
        scratch = {"both": ((2 * part, width), BF16), "embeds": ((2 * part, emb), BF16)}
        if step < k:
            outs = {**outs, "embed": embed_shape, "sq_rem": sq_shape, "sq_rs": sq_shape}
            outs["token"] = ((8, 128), F32)
            for name in names_of(step, "rem") + [("rem", step)]:
                outs["summed", name] = ((tok if name == 0 else part, emb), F32)
            out = run(functools.partial(rs_stage, step), ins, outs, scratch)
            token = out["token"]
            for name in names_of(step, "rem") + [("rem", step)]:
                summed[name] = out["summed", name]
            name = ("rs", step)
            feats[name], embed[name], sq[name] = out["feats"], out["embed"], out["sq_rs"]
            sq["rem", step] = out["sq_rem"]
    rows = {}
    for j in range(k + 1):
        rows["hidden", j] = hidden[j]
        rows["gate", j] = gate[j]
    out = run(
        functools.partial(last_stage, factor),
        {**ins, **rows},
        {
            "dembed": ((2 * tok, emb), BF16),
            "give": ((256, 2 * tok), BF16),
        },
        scratch,
    )
    feats["rs", k] = rs[0]
    got = blk_swap(out["give"], 1)
    mine = {("feats", n): feats[n] for n in (0, ("rem", 0), ("rem", k))}
    theirs = {("feats", n): feats[n] for n in (0, ("rs", 0), ("rs", k))}
    dembed = out["dembed"]
    own = run(
        own_share,
        {"w_second": w_second, "dembed": dembed, **rows, **mine},
        {
            "keep": ((256, 2 * tok), BF16),
            "second_give": ((emb // 4, hid), F32),
            "first": ((4, CUT, 256), F32),
        },
        {},
    )
    second_got = blk_swap(own["second_give"], 1)
    out = run(
        first_gradients,
        {"keep": own["keep"], "got": got, "first": own["first"], **theirs},
        {"one": ((4, rows_one, 256), F32), "exp_first": ((8, 256), F32)},
        {},
    )
    one_give = out["one"]
    more = extra.bit_length() - 1
    shape = (2,) * more
    kind_one, kind_two = kinds[0][:, :lanes], kinds[1][:, :lanes]
    shifts = [more + 1, more] + [more - 1 - n for n in range(more)]
    rest = list(range(2, more + 2))
    cut = functools.partial(split_lanes, bounds=(0, 0), count=extra)
    one_give = cut(one_give).reshape((4,) + shape + (rows_one, lanes))
    early = encode16(one_give, kind_one, rows_one - 16)
    got, early = lax.optimization_barrier((got, early))
    ins = {"keep": own["keep"], "got": got, "exp_first": out["exp_first"], **mine, **theirs}
    out = run(
        second_gradients,
        {
            **ins,
            "dembed": dembed,
            "second_got": second_got,
            **{n: v for n, v in rows.items() if n[0] == "hidden"},
        },
        {"two": ((8, rows_two, 256), F32)},
        {"second": ((emb // 4, hid), F32)},
    )
    two = split_lanes(out["two"], (256 - CUT, 320 - CUT), extra)
    two = Sum(two.reshape((4, 2) + shape + (rows_two, lanes)), kind_two, [0] + rest + [1], 2)
    packs_two = two.pack(0, shifts)
    ins["got"], packs_two = lax.optimization_barrier((got, packs_two))
    kept = run(kept_gradients, ins, {"one": ((4, rows_one, 256), F32)}, {})
    one_keep = cut(kept["one"]).reshape(one_give.shape)
    one = Sum(jnp.stack([one_keep, one_give], 1), kind_one, [1, 0] + rest, 2, (one_keep, one_give))
    one.pack(0, shifts)
    gots_one = one.swap(0, shifts, [early])
    gots_two = two.swap(0, shifts, packs_two)
    for step in range(1, more + 2):
        one.receive(gots_one)
        packs = one.pack(step, shifts)
        gots_two, packs = lax.optimization_barrier((gots_two, packs))
        gots_one = one.swap(step, shifts, packs)
        gots_two, gots_one[0] = lax.optimization_barrier((gots_two, gots_one[0]))
        two.receive(gots_two)
        gots_two = two.swap(step, shifts, two.pack(step, shifts))
    one.receive(gots_one)
    two.receive(gots_two)
    if extra == 1:
        out = run(
            turn_quarter,
            {"one": one.total, "two": two.total},
            {"all": ((336, 256), F32)},
            {},
        )
        four = [out["all"]]
        four += [decode16(g, kinds[2], 320) for g in gather(encode16(out["all"], kinds[2], 320))[1:]]
        out = run(
            place_quarters,
            {("all", j): v for j, v in enumerate(four)},
            {"first": ((lanes, hid), F32), "second": ((lanes // 2, emb), F32)},
            {"sems": pltpu.SemaphoreType.DMA((12,))},
            to_hbm=True,
        )
        return out["first"], out["second"]
    packed = [encode16(one.total, kind_one, one.tail), encode16(two.total, kind_two, two.tail)]
    every = jnp.stack(gather(jnp.concatenate(packed, 0)))
    one = decode16(every[:, :rows_one], kind_one, one.tail)
    two = decode16(every[:, rows_one:], kind_two, two.tail)
    order = jnp.arange(4) ^ lax.axis_index("blk")
    first = jnp.concatenate([one[:, :CUT], two[:, : 256 - CUT]], 1)[order].reshape(hid, lanes)
    second = two[order, 256 - CUT : 320 - CUT]
    second = jnp.concatenate([second[..., : lanes // 2], second[..., lanes // 2 :]], 1)
    return first.T, second.reshape(emb, lanes // 2).T


def gather(packed):
    across = blk_swap(packed, 2)
    pair = jnp.stack([packed, across])
    beside = blk_swap(pair, 1)
    return [packed, beside[0], across, beside[1]]


def solution(mesh):
    in_specs = (P(("blk", "dp"), None), P(), P())
    out_specs = (P("dp", None), P("dp", None))
    return jax.shard_map(
        per_device, mesh=mesh, in_specs=in_specs, out_specs=out_specs, check_vma=False
    )
```
